256 devices in a mesh: ctx: 32 (over x, z), head: 8 (over y, core).
Axes of the slice: x: 4, y: 4, z: 8, core: 2. Of those that a mesh axis runs over, the one named last changes fastest.
Arguments:
- inputs: bfloat16 [16384, 8192], P(('ctx', 'head')), may hold values from -1.75 to 1.75
- grad_out: bfloat16 [16384, 8192], P(('ctx', 'head')), may hold values from -1.75 to 1.75
- steps: bfloat16 [16384, 128], P(('ctx', 'head')), may hold values from 0.049804688 to 0.19921875
- log_decay: bfloat16 [16384, 128], P(('ctx', 'head')), may hold values from -0.52 to 0
- input_map: bfloat16 [16384, 128], P(('ctx', 'head')), may hold values from -0.5 to 0.5
- output_map: bfloat16 [16384, 128], P(('ctx', 'head')), may hold values from -0.5 to 0.5
- skip_gain: float32 [128], P('head'), may hold values from 0.5 to 1.5
Outputs:
- grad_inputs: bfloat16 [16384, 8192], P(('ctx', 'head'))
- grad_steps: bfloat16 [16384, 128], P(('ctx', 'head'))
- grad_decay: bfloat16 [16384, 128], P(('ctx', 'head'))
- grad_input_map: float32 [16384, 128], P(('ctx', 'head'))
- grad_output_map: float32 [16384, 128], P(('ctx', 'head'))
The draws below stay inside these ranges and needn't reach their ends.
All inputs are finite; a program needn't handle non-finite values.
Results may differ from the reference program's by a relative error of at most 0.004.
Values may be sent and summed in bfloat16 or wider, within the bound.
A program may use at most 128 MiB of HBM per device.

```python
import math
import jax
import jax.numpy as jnp
from jax import lax

HEADS = 128
HEAD_DIM = 64
STATE = 128
SPAN = 256
L_DEV = 512
INNER = 8192
TOKENS = 16384


def draw_log_decay(key, part):
    key_kind, key_fast, key_slow, key_rough, key_block, key_spot, key_loss = jax.random.split(key, 7)
    slow_share = 0.5
    slow_head = jax.random.uniform(key_kind, (HEADS,)) < slow_share
    fast_rate = jnp.exp(jax.random.uniform(key_fast, (HEADS,), minval=jnp.log(1.0 / 50.0), maxval=jnp.log(1.0 / 30.0)))
    slow_rate = jnp.exp(jax.random.uniform(key_slow, (HEADS,), minval=jnp.log(0.1), maxval=jnp.log(0.5))) / TOKENS
    head_rate_value = jnp.where(slow_head, slow_rate, fast_rate)
    coarse_estimate = jnp.exp(jax.random.uniform(key_rough, (TOKENS, HEADS), minval=jnp.log(0.5), maxval=jnp.log(2.0)))
    block_factor = jnp.exp(jax.random.uniform(key_block, (TOKENS // L_DEV, HEADS), minval=jnp.log(0.5), maxval=jnp.log(2.0)))
    block_complete = jnp.repeat(block_factor, L_DEV, axis=0)
    sample_locations = jax.random.randint(key_spot, (2,), 0, TOKENS)
    token_positions = lax.broadcasted_iota(jnp.int32, (TOKENS, 1), 0)
    sudden_spike = jnp.any(token_positions == sample_locations[None, :], axis=1)
    retained_items = jax.random.uniform(key_loss, (TOKENS, HEADS), minval=0.6, maxval=0.8)
    value_rows = jnp.where(sudden_spike[:, None], jnp.log(retained_items), -head_rate_value[None, :] * coarse_estimate * block_complete)
    return value_rows.astype(jnp.bfloat16)


def levels(own_key, dims, cuts, smallest, largest):
    loudness = 1.0
    for dim, blocks in cuts:
        draws = jax.random.uniform(jax.random.fold_in(jax.random.fold_in(own_key, 6), dim), (blocks,), jnp.float32, smallest / len(cuts), largest / len(cuts))
        loudness = loudness * jnp.repeat(jnp.exp(draws), dims[dim] // blocks).reshape((-1,) + (1,) * (len(dims) - 1 - dim))
    return loudness


def noise(stream_key, shape, deviation, most, cuts=(), kind=jnp.bfloat16):
    values = jax.random.normal(stream_key, shape, jnp.float32) * deviation
    if len(cuts) > 0:
        values = levels(stream_key, shape, cuts, -0.22, 0.18) * values
    return jnp.clip(values, min=-most, max=most).astype(kind)


def setup_inputs(seed: int = 0) -> dict:
    keys = jax.random.split(jax.random.key(seed), 8)
    inputs = noise(keys[0], (TOKENS, INNER), 0.3, 1.75, ((0, 256),))
    grad_out = noise(keys[1], (TOKENS, INNER), 0.3, 1.75, ((0, 256),))
    steps = jnp.clip(jnp.exp(math.log(0.19921875) - 1.3862944 * jax.random.uniform(keys[2], (TOKENS, HEADS), jnp.float32) ** levels(keys[2], (TOKENS, HEADS), ((0, 256),), -0.2, 0.2)), 0.049804688, 0.19921875).astype(jnp.bfloat16)
    log_decay = draw_log_decay(jax.random.fold_in(keys[7], 71), 0)
    input_map = noise(keys[4], (TOKENS, STATE), STATE ** -0.5, 0.5, ((0, 256),))
    output_map = noise(keys[5], (TOKENS, STATE), STATE ** -0.5, 0.5, ((0, 256),))
    skip_gain = jnp.clip(0.5 + 1.0 * jax.random.uniform(keys[6], (HEADS,), jnp.float32) ** levels(keys[6], (HEADS,), ((0, 8),), -0.2, 0.2), 0.5, 1.5)
    return dict(inputs=inputs, grad_out=grad_out, steps=steps, log_decay=log_decay, input_map=input_map, output_map=output_map, skip_gain=skip_gain)


def local_forward(value_rows, step_sizes, log_steps, key_rows, query_rows, skip_local, start_state, span_len):
    length, groups, head_width = value_rows.shape
    blocks = length // span_len
    highest = lax.Precision.HIGHEST
    plain = lax.Precision.DEFAULT
    scaled = (value_rows * step_sizes[:, :, None]).reshape(blocks, span_len, groups, head_width)
    cumlog = jnp.cumsum(log_steps.reshape(blocks, span_len, groups).transpose(0, 2, 1), axis=2)
    row_index = lax.broadcasted_iota(jnp.int32, (span_len, span_len), 0)
    col_index = lax.broadcasted_iota(jnp.int32, (span_len, span_len), 1)
    below_diag = row_index >= col_index
    spread = cumlog[:, :, :, None] - cumlog[:, :, None, :]
    decays = jnp.exp(jnp.where(below_diag, spread, 0.0)) * below_diag.astype(jnp.float32)
    keys_blk = key_rows.reshape(blocks, span_len, key_rows.shape[1])
    queries_blk = query_rows.reshape(blocks, span_len, query_rows.shape[1])
    intersection = jnp.einsum('cqn,ckn->cqk', queries_blk, keys_blk, precision=plain)
    scores = intersection[:, None, :, :] * decays
    diag_out = jnp.einsum('cgqk,ckgp->cqgp', scores, scaled, precision=highest)
    to_end = jnp.exp(cumlog[:, :, -1:] - cumlog)
    weighted = scaled * to_end.transpose(0, 2, 1)[:, :, :, None]
    block_states = jnp.einsum('ckn,ckgp->cgpn', keys_blk, weighted, precision=highest)
    block_decay = jnp.exp(cumlog[:, :, -1])

    def advance(carry_state, link_pair):
        decay_now, added_state = link_pair
        return (decay_now[:, None, None] * carry_state + added_state, carry_state)
    final_state, start_states = lax.scan(advance, start_state, (block_decay, block_states))
    carried = jnp.einsum('cqn,cgpn->cqgp', queries_blk, start_states, precision=highest)
    carried = carried * jnp.exp(cumlog).transpose(0, 2, 1)[:, :, :, None]
    outputs = (diag_out + carried).reshape(length, groups, head_width) + skip_local[None, :, None] * value_rows
    return (outputs, final_state)

def reference(inputs, grad_out, steps, log_decay, input_map, output_map, skip_gain):
    token_count = inputs.shape[0]
    group_size = 8
    group_count = HEADS // group_size
    group_inputs = inputs.astype(jnp.float32).reshape(token_count, group_count, group_size, HEAD_DIM).transpose(1, 0, 2, 3)
    group_cotan = grad_out.astype(jnp.float32).reshape(token_count, group_count, group_size, HEAD_DIM).transpose(1, 0, 2, 3)
    group_steps = steps.astype(jnp.float32).reshape(token_count, group_count, group_size).transpose(1, 0, 2)
    group_decay = log_decay.astype(jnp.float32).reshape(token_count, group_count, group_size).transpose(1, 0, 2)
    group_skip = skip_gain.reshape(group_count, group_size)
    key_rows = input_map.astype(jnp.float32)
    query_rows = output_map.astype(jnp.float32)
    zero_state = jnp.zeros((group_size, HEAD_DIM, STATE), jnp.float32)

    def per_group(running, pieces):
        piece_inputs, piece_cotan, piece_steps, piece_decay, piece_skip = pieces

        def forward(value_rows, step_sizes, log_steps, keys_in, queries_in):
            return local_forward(value_rows, step_sizes, log_steps, keys_in, queries_in, piece_skip, zero_state, SPAN)[0]
        unused, pullback = jax.vjp(forward, piece_inputs, piece_steps, piece_decay, key_rows, query_rows)
        grad_values, grad_sizes, grad_logs, grad_keys, grad_queries = pullback(piece_cotan)
        return ((running[0] + grad_keys, running[1] + grad_queries), (grad_values, grad_sizes, grad_logs))
    start = (jnp.zeros((token_count, STATE), jnp.float32), jnp.zeros((token_count, STATE), jnp.float32))
    sums, stacked = lax.scan(per_group, start, (group_inputs, group_cotan, group_steps, group_decay, group_skip))
    grad_values, grad_sizes, grad_logs = stacked
    grad_inputs = grad_values.transpose(1, 0, 2, 3).reshape(token_count, HEADS * HEAD_DIM).astype(jnp.bfloat16)
    grad_steps = grad_sizes.transpose(1, 0, 2).reshape(token_count, HEADS).astype(jnp.bfloat16)
    grad_decay = grad_logs.transpose(1, 0, 2).reshape(token_count, HEADS).astype(jnp.bfloat16)
    return (grad_inputs, grad_steps, grad_decay, sums[0], sums[1])
```

```python
import jax
import jax.numpy as jnp
from jax import lax
from jax.experimental import pallas as pl
from jax.experimental.pallas import tpu as pltpu
from jax.sharding import PartitionSpec as P

BF = jnp.bfloat16
F32 = jnp.float32
MESH = pl.DeviceIdType.MESH
NC = 32
NH = 8
TOK = 64
LEN = 512
Q = 128
CH = LEN // Q
W = 1024
HD = 64
N = 128
GH = 16
RB = 32
SOUT = F32
SBACK = BF
GOUT = BF
GBACK = BF

NN = ((1,), (0,))
NT = ((1,), (1,))


def dot(a, b, dims=NN):
    return lax.dot_general(a, b, (dims, ((), ())), preferred_element_type=F32)


def halves(a):
    hi = a.astype(BF)
    return hi, (a - hi.astype(F32)).astype(BF)


def iota(shape, axis):
    return lax.broadcasted_iota(jnp.int32, shape, axis)


def ones_where(cond):
    return jnp.where(cond, 1.0, 0.0).astype(BF)


def kernel(
    x, g, st, ld, bm, cm, skip, ox, ods, odq, ogb, ogc,
    gb, xb, sm, rep, f1, f2, f1d, f2d, rowf, tri, stc, cumc, ct2, bt2, gx, xs,
    lg, ls, acc, v, dxb, gin, sin, dec, decr, gs, gr, gbs, gbr, ss, sr, sbs, sbr,
    cs, rs, prod, gbp, gcp, gbrv, gcrv, pk, pkr, send, recv,
):
    me_c = lax.axis_index("ctx")
    me_h = lax.axis_index("head")

    def cpeer(r):
        return lax.rem(me_c + r, NC)

    def hpeer(r):
        return lax.rem(me_h + r, NH)

    def remote(src, dst, s, axis, to):
        pltpu.make_async_remote_copy(
            src_ref=src, dst_ref=dst, send_sem=send.at[s], recv_sem=recv.at[s],
            device_id={axis: to}, device_id_type=MESH,
        ).start()

    def local(src, dst, s):
        pltpu.make_async_copy(src, dst, recv.at[s]).start()

    def arrived(ref, s):
        pltpu.make_async_copy(ref, ref, recv.at[s]).wait()

    def left(ref, s):
        pltpu.make_async_copy(ref, ref, send.at[s]).wait()

    barrier = pltpu.get_barrier_semaphore()

    def greet_head(r, z):
        pl.semaphore_signal(barrier, inc=1, device_id={"head": hpeer(r)}, device_id_type=MESH)
        return z

    def greet_ctx(r, z):
        pl.semaphore_signal(barrier, inc=1, device_id={"ctx": cpeer(r)}, device_id_type=MESH)
        return z

    lax.fori_loop(1, NH, greet_head, 0)
    lax.fori_loop(1, NC, greet_ctx, 0)
    pl.semaphore_wait(barrier, NH + NC - 2)

    mine = pl.ds(pl.multiple_of(me_h * TOK, TOK), TOK)

    def cols(k):
        return pl.ds(pl.multiple_of(k * W, W), W)

    def send_small(r, z):
        to = hpeer(r)
        for a, src in enumerate((bm, cm, st, ld)):
            remote(src, sm.at[a, mine, :], 0, "head", to)
        return z

    def send_g(r, z):
        to = hpeer(r)
        remote(g.at[:, cols(to)], gb.at[mine, :], 1, "head", to)
        return z

    def send_x(r, z):
        to = hpeer(r)
        remote(x.at[:, cols(to)], xb.at[mine, :], 2, "head", to)
        return z

    lax.fori_loop(1, NH, send_small, 0)
    for a, src in enumerate((bm, cm, st, ld)):
        local(src, sm.at[a, mine, :], 0)
    lax.fori_loop(1, NH, send_g, 0)
    local(g.at[:, cols(me_h)], gb.at[mine, :], 1)
    lax.fori_loop(1, NH, send_x, 0)
    local(x.at[:, cols(me_h)], xb.at[mine, :], 2)

    rep_one = ones_where(iota((N, W), 0) == iota((N, W), 1) // HD)
    rep[0:N, :] = rep_one
    rep[N : 2 * N, :] = rep_one
    row, col = iota((Q, Q), 0), iota((Q, Q), 1)
    tri[...] = ones_where(row >= col)
    below = row >= col
    above = row <= col
    pick = ones_where((row == me_h * GH + col) & (col < GH))

    arrived(sm, 0)

    stc[...] = dot(sm[2], pick)
    lds = dot(sm[3], pick).astype(BF)
    tots = []
    for c in range(CH):
        cum = dot(tri[...], lds[c * Q : (c + 1) * Q, :])
        cumc[c * Q : (c + 1) * Q, :] = cum
        tots.append(cum[Q - 1 : Q, :])
    upto = [tots[0]]
    for c in range(1, CH):
        upto.append(upto[-1] + tots[c])
    beyond = [None] * CH
    beyond[CH - 1] = jnp.zeros_like(tots[0])
    for c in range(CH - 2, -1, -1):
        beyond[c] = beyond[c + 1] + tots[c + 1]
    for k in range(CH):
        prod[k : k + 1, 0:N] = tots[k]
        prod[CH + k : CH + k + 1, 0:N] = upto[k]
        prod[2 * CH + k : 2 * CH + k + 1, 0:N] = beyond[k]
        prod[3 * CH + k : 3 * CH + k + 1, 0:N] = jnp.zeros_like(tots[0])
    rows = jnp.exp(prod[:, 0:N])
    hi, rest = rows.astype(BF), rows - rows.astype(BF).astype(F32)
    mid, low = halves(rest)
    rowf[...] = dot(jnp.concatenate([hi, mid], axis=1), rep[...]) + dot(low, rep[0:N, :])
    dec[...] = jnp.broadcast_to(rowf[2 * CH - 1 : 2 * CH, :], (8, W))

    def send_decay(r, z):
        k = cpeer(r)
        remote(dec.at[:, pl.ds(pl.multiple_of(k // 4 * N, N), N)], decr.at[me_c], 3, "ctx", k)
        return z

    lax.fori_loop(1, NC, send_decay, 0)
    local(dec.at[:, pl.ds(pl.multiple_of(me_c // 4 * N, N), N)], decr.at[me_c], 3)

    def chunk(c):
        return pl.ds(pl.multiple_of(c * Q, Q), Q)

    def expand(a):
        return dot(jnp.concatenate(halves(a), axis=1), rep[...])

    def transposed(a, out, c):
        t = jnp.transpose(a.astype(F32)).astype(BF)
        out[c, :, 0:Q] = t
        out[c, :, Q : 2 * Q] = t

    for c in range(CH):
        at = slice(c * Q, (c + 1) * Q)
        cum = cumc[at, :]
        s = stc[at, :]
        f1[at, :] = expand(jnp.exp(cum))
        f2[at, :] = expand(s * jnp.exp(-cum))
        f1d[at, :] = expand(jnp.exp(cum + (upto[c] - tots[c])))
        f2d[at, :] = expand(s * jnp.exp(tots[c] - cum + beyond[c]))
        transposed(sm[0, at, :], bt2, c)
        transposed(sm[1, at, :], ct2, c)
    skip_hi = skip[...].astype(BF)
    skip_rest = skip[...] - skip_hi.astype(F32)
    skip_mid, skip_low = halves(skip_rest)
    skip_row = (
        dot(skip_hi, rep[0:GH, :]) + dot(skip_mid, rep[0:GH, :]) + dot(skip_low, rep[0:GH, :])
    )

    arrived(gb, 1)
    acc[...] = jnp.zeros_like(acc)

    def step_g(r, z):
        c = CH - 1 - r
        at = chunk(c)
        ghi, glo = halves(gb[at, :].astype(F32) * f1[at, :])
        gx[c, 0:Q, :] = ghi
        end = acc[...]
        lg[c] = end
        end = end * rowf[pl.ds(c, 1), :]
        gx[c, Q : 2 * Q, :] = end.astype(BF)
        acc[...] = end + dot(ct2[c], jnp.concatenate([ghi, glo], axis=0))
        return z

    lax.fori_loop(0, CH, step_g, 0)

    def stage(src, dst):
        for k in range(NC):
            a, b = k % 4 * RB, k // 4 * N
            dst[k] = src[a : a + RB, b : b + N].astype(dst.dtype)

    def unstage(src, dst):
        for k in range(NC):
            a, b = k % 4 * RB, k // 4 * N
            dst[a : a + RB, b : b + N] = src[k].astype(dst.dtype)

    def spread(src, dst, s):
        def one(r, z):
            k = cpeer(r)
            remote(src.at[k], dst.at[me_c], s, "ctx", k)
            return z

        lax.fori_loop(1, NC, one, 0)
        local(src.at[me_c], dst.at[me_c], s)

    stage(acc, gs)
    spread(gs, gr, 4)

    def step_u(c, z):
        at = chunk(c)
        b = sm[0, at, :]
        cb = jnp.where(above, dot(b, sm[1, at, :], NT), 0.0).astype(BF)
        v[at, :] = f2[at, :] * dot(jnp.concatenate([cb, b], axis=1), gx[c])
        return z

    lax.fori_loop(0, CH, step_u, 0)

    arrived(decr, 3)
    arrived(gr, 4)

    def back_g(r, carry):
        i = NC - 1 - r
        gbs[i] = carry.astype(gbs.dtype)
        return carry * decr[i][0:1, :] + gr[i].astype(F32)

    lax.fori_loop(0, NC, back_g, jnp.zeros((RB, N), F32))
    spread(gbs, gbr, 5)

    arrived(xb, 2)
    acc[...] = jnp.zeros_like(acc)

    def step_x(c, z):
        at = chunk(c)
        xhi, xlo = halves(xb[at, :].astype(F32) * f2[at, :])
        xs[c, 0:Q, :] = xhi
        start = acc[...]
        ls[c] = start
        xs[c, Q : 2 * Q, :] = start.astype(BF)
        more = dot(bt2[c], jnp.concatenate([xhi, xlo], axis=0))
        acc[...] = (start + more) * rowf[pl.ds(c, 1), :]
        return z

    lax.fori_loop(0, CH, step_x, 0)
    ls[CH] = acc[...]
    stage(acc, ss)
    spread(ss, sr, 6)

    arrived(gbr, 5)
    unstage(gbr, gin)

    def block(k):
        return pl.ds(pl.multiple_of(k * TOK, TOK), TOK)

    def make_dx(p):
        at = chunk(p)
        now = v[at, :] + f2d[at, :] * dot(sm[0, at, :], gin[...])
        v[at, :] = now
        dxb[at, :] = (now + skip_row * gb[at, :].astype(F32)).astype(BF)

    def send_dx(to):
        remote(dxb.at[block(to), :], ox.at[:, cols(me_h)], 7, "head", to)

    def step_dx(r, z):
        p = lax.rem(me_h // 2 + r, NH // 2)
        make_dx(p)
        send_dx(2 * p)
        send_dx(2 * p + 1)
        return z

    lax.fori_loop(1, NH // 2, step_dx, 0)
    make_dx(me_h // 2)
    send_dx(me_h + 1 - 2 * lax.rem(me_h, 2))
    local(dxb.at[block(me_h), :], ox.at[:, cols(me_h)], 7)

    arrived(sr, 6)

    def back_s(i, carry):
        sbs[i] = carry.astype(sbs.dtype)
        return carry * decr[i][0:1, :] + sr[i].astype(F32)

    lax.fori_loop(0, NC, back_s, jnp.zeros((RB, N), F32))
    spread(sbs, sbr, 8)

    def heads_sum(a):
        hi, lo = halves(a)
        return dot(hi, rep[0:N, :], NT) + dot(lo, rep[0:N, :], NT)

    def step_local(c, z):
        at = chunk(c)
        b, cc = sm[0, at, :], sm[1, at, :]
        gh, xh = gx[c, 0:Q, :], xs[c, 0:Q, :]
        xf, gf = xb[at, :].astype(F32), gb[at, :].astype(F32)
        cs[at, :] = heads_sum(xf * v[at, :])
        e = jnp.where(below, dot(gh, xh, NT), 0.0).astype(BF)
        et = jnp.where(above, dot(xh, gh, NT), 0.0).astype(BF)
        gbp[at, :] = (
            dot(et, cc)
            + dot(xh, gx[c, Q : 2 * Q, :], NT)
            + dot((xf * f2d[at, :]).astype(BF), gin[...], NT)
        )
        gcp[at, :] = dot(e, b) + dot(gh, xs[c, Q : 2 * Q, :], NT)
        cb = jnp.where(below, dot(cc, b, NT), 0.0).astype(BF)
        y = f1[at, :] * dot(jnp.concatenate([cb, cc], axis=1), xs[c])
        rs[at, :] = heads_sum(gf * y)
        return z

    lax.fori_loop(0, CH, step_local, 0)

    def share(src, dst, s):
        def one(r, z):
            to = hpeer(r)
            remote(src.at[block(to), :], dst.at[me_h], s, "head", to)
            return z

        lax.fori_loop(1, NH, one, 0)
        local(src.at[block(me_h), :], dst.at[me_h], s)

    share(gbp, gbrv, 9)

    arrived(sbr, 8)
    unstage(sbr, sin)

    def step_s(c, z):
        at = chunk(c)
        gf = gb[at, :].astype(F32)
        gd = gf * f1d[at, :]
        gcp[at, :] = gcp[at, :] + dot(gd.astype(BF), sin[...], NT)
        rs[at, :] = rs[at, :] + heads_sum(gd * dot(sm[1, at, :], sin[...]))
        return z

    lax.fori_loop(0, CH, step_s, 0)
    share(gcp, gcrv, 10)

    prod[...] = jnp.zeros_like(prod)
    for c in range(CH):
        ge = lg[c] + rowf[2 * CH + c : 2 * CH + c + 1, :] * gin[...].astype(F32)
        se = ls[c + 1] + rowf[CH + c : CH + c + 1, :] * sin[...].astype(F32)
        prod[c : c + 1, :] = jnp.sum(ge * se, axis=0, keepdims=True)
    base = heads_sum(prod[...])
    lane = iota((Q, N), 1)
    upper = ones_where(above)
    for c in range(CH):
        at = slice(c * Q, (c + 1) * Q)
        csum = cs[at, :]
        hi, lo = halves(rs[at, :] - csum)
        dq = base[c : c + 1, :] + dot(upper, hi) + dot(upper, lo)
        ds = jnp.where(lane < GH, csum / jnp.where(lane < GH, stc[at, :], 1.0), 0.0)
        pk[at, :] = (ds + pltpu.roll(dq, GH, 1)).astype(BF)

    def send_pk(r, z):
        to = hpeer(r)
        remote(pk.at[block(to), :], pkr.at[:, pl.ds(pl.multiple_of(me_h * N, N), N)], 11, "head", to)
        return z

    lax.fori_loop(1, NH, send_pk, 0)
    local(pk.at[block(me_h), :], pkr.at[:, pl.ds(pl.multiple_of(me_h * N, N), N)], 11)

    arrived(gbrv, 9)
    ogb[...] = jnp.sum(gbrv[...], axis=0)
    arrived(gcrv, 10)
    ogc[...] = jnp.sum(gcrv[...], axis=0)
    arrived(pkr, 11)
    a, b = iota((W, N), 0), iota((W, N), 1)
    want = b // GH * N + b - b // GH * GH
    ods[...] = dot(pkr[...], ones_where(a == want)).astype(BF)
    odq[...] = dot(pkr[...], ones_where(a == want + GH)).astype(BF)
    arrived(ox, 7)

    left(sm.at[:, pl.ds(0, LEN - TOK), :], 0)
    left(gb.at[pl.ds(0, LEN - TOK), :], 1)
    left(xb.at[pl.ds(0, LEN - TOK), :], 2)
    left(decr.at[pl.ds(0, NC - 1)], 3)
    left(gs.at[pl.ds(0, NC - 1)], 4)
    left(gbs.at[pl.ds(0, NC - 1)], 5)
    left(ss.at[pl.ds(0, NC - 1)], 6)
    left(dxb.at[pl.ds(0, LEN - TOK), :], 7)
    left(sbs.at[pl.ds(0, NC - 1)], 8)
    left(gbp.at[pl.ds(0, LEN - TOK), :], 9)
    left(gcp.at[pl.ds(0, LEN - TOK), :], 10)
    left(pk.at[pl.ds(0, LEN - TOK), :], 11)


def body(inputs, grad_out, steps, log_decay, input_map, output_map, skip_gain):
    hbm = pl.BlockSpec(memory_space=pl.ANY)
    vmem = pl.BlockSpec(memory_space=pltpu.VMEM)

    def vm(shape, kind):
        return pltpu.VMEM(shape, kind)

    grads = pl.pallas_call(
        kernel,
        out_shape=(
            jax.ShapeDtypeStruct((TOK, NH * W), BF),
            jax.ShapeDtypeStruct((TOK, N), BF),
            jax.ShapeDtypeStruct((TOK, N), BF),
            jax.ShapeDtypeStruct((TOK, N), F32),
            jax.ShapeDtypeStruct((TOK, N), F32),
        ),
        in_specs=[hbm] * 6 + [vmem],
        out_specs=(hbm, vmem, vmem, vmem, vmem),
        scratch_shapes=[
            vm((LEN, W), BF),
            vm((LEN, W), BF),
            vm((4, LEN, N), BF),
            vm((2 * N, W), BF),
            vm((LEN, W), F32),
            vm((LEN, W), F32),
            vm((LEN, W), F32),
            vm((LEN, W), F32),
            vm((4 * CH, W), F32),
            vm((Q, Q), BF),
            vm((LEN, N), F32),
            vm((LEN, N), F32),
            vm((CH, N, 2 * Q), BF),
            vm((CH, N, 2 * Q), BF),
            vm((CH, 2 * Q, W), BF),
            vm((CH, 2 * Q, W), BF),
            vm((CH, N, W), F32),
            vm((CH + 1, N, W), F32),
            vm((N, W), F32),
            vm((LEN, W), F32),
            vm((LEN, W), BF),
            vm((N, W), BF),
            vm((N, W), BF),
            vm((8, W), F32),
            vm((NC, 8, N), F32),
            vm((NC, RB, N), GOUT),
            vm((NC, RB, N), GOUT),
            vm((NC, RB, N), GBACK),
            vm((NC, RB, N), GBACK),
            vm((NC, RB, N), SOUT),
            vm((NC, RB, N), SOUT),
            vm((NC, RB, N), SBACK),
            vm((NC, RB, N), SBACK),
            vm((LEN, N), F32),
            vm((LEN, N), F32),
            vm((4 * CH, W), F32),
            vm((LEN, N), F32),
            vm((LEN, N), F32),
            vm((NH, TOK, N), F32),
            vm((NH, TOK, N), F32),
            vm((LEN, N), BF),
            vm((TOK, NH * N), BF),
            pltpu.SemaphoreType.DMA((12,)),
            pltpu.SemaphoreType.DMA((12,)),
        ],
        compiler_params=pltpu.CompilerParams(
            collective_id=0, has_side_effects=True, vmem_limit_bytes=56 * 1024 * 1024
        ),
        cost_estimate=pl.CostEstimate(
            flops=3 * 10**9, bytes_accessed=8 * 2**20, transcendentals=2**20
        ),
        name="block_backward",
    )(inputs, grad_out, steps, log_decay, input_map, output_map, skip_gain.reshape(1, GH))
    return grads


def solution(mesh):
    spread = P(("ctx", "head"), None)
    return jax.shard_map(
        body,
        mesh=mesh,
        in_specs=(spread,) * 6 + (P("head"),),
        out_specs=(spread,) * 5,
        check_vma=False,
    )
```

```python
import jax
import jax.numpy as jnp
from jax import lax
from jax.experimental import pallas as pl
from jax.experimental.pallas import tpu as pltpu
from jax.sharding import PartitionSpec as P

BF = jnp.bfloat16
F32 = jnp.float32
MESH = pl.DeviceIdType.MESH
NC = 32
NH = 8
TOK = 64
LEN = 512
Q = 128
CH = LEN // Q
W = 1024
HD = 64
N = 128
GH = 16
HW = W // 2
RB = 16
RG = N // RB
LG = HW // N
CHIPS = NH // 2

NN = ((1,), (0,))
NT = ((1,), (1,))


def dot(a, b, dims=NN):
    return lax.dot_general(a, b, (dims, ((), ())), preferred_element_type=F32)


def halves(a):
    hi = a.astype(BF)
    return hi, (a - hi.astype(F32)).astype(BF)


def iota(shape, axis):
    return lax.broadcasted_iota(jnp.int32, shape, axis)


def ones_where(cond):
    return jnp.where(cond, 1.0, 0.0).astype(BF)


def kernel(
    x, g, st, ld, bm, cm, skip, ox, ods, odq, ogb, ogc,
    gb, xb, sm, own, pki, pkr, rep, f1, f2, f1d, f2d, rowf, tri, stc, cumc, ct2, bt2, gx, xs,
    lg, ls, acc, v, dxb, gin, sin, dec, decr, gs, gr, gbs, gbr, gf32, ss, sr, sbs, sbr, pairs, pairr,
    cs, rs, prod, gbp, gcp, gbo, gco, gbh, gch, gbrv, gcrv, pko, pkv, send, recv,
):
    me_c = lax.axis_index("ctx")
    me_h = lax.axis_index("head")
    core = lax.rem(me_h, 2)
    chip = me_h // 2
    sibling = me_h + 1 - 2 * core

    def cpeer(r):
        return lax.rem(me_c + r, NC)

    def hpeer(r):
        return lax.rem(me_h + r, NH)

    def remote(src, dst, s, axis, to):
        pltpu.make_async_remote_copy(
            src_ref=src, dst_ref=dst, send_sem=send.at[s], recv_sem=recv.at[s],
            device_id={axis: to}, device_id_type=MESH,
        ).start()

    def local(src, dst, s):
        pltpu.make_async_copy(src, dst, recv.at[s]).start()

    def arrived(ref, s):
        pltpu.make_async_copy(ref, ref, recv.at[s]).wait()

    def left(ref, s):
        pltpu.make_async_copy(ref, ref, send.at[s]).wait()

    def block(k):
        return pl.ds(pl.multiple_of(k * TOK, TOK), TOK)

    def heads(k):
        return pl.ds(pl.multiple_of(k * GH, GH), GH)

    barrier = pltpu.get_barrier_semaphore()

    def greet_head(r, z):
        pl.semaphore_signal(barrier, inc=1, device_id={"head": hpeer(r)}, device_id_type=MESH)
        return z

    def greet_ctx(r, z):
        pl.semaphore_signal(barrier, inc=1, device_id={"ctx": cpeer(r)}, device_id_type=MESH)
        return z

    lax.fori_loop(1, NH, greet_head, 0)
    lax.fori_loop(1, NC, greet_ctx, 0)

    local(st, own.at[pl.ds(0, TOK), :], 24)
    local(ld, own.at[pl.ds(TOK, TOK), :], 24)
    rep_one = ones_where(iota((N, W), 0) == iota((N, W), 1) // HD)
    rep[0:N, :] = rep_one
    rep[N : 2 * N, :] = rep_one
    row, col = iota((Q, Q), 0), iota((Q, Q), 1)
    tri[...] = ones_where(row >= col)
    below = row >= col
    above = row <= col
    skip_hi = skip[...].astype(BF)
    skip_mid, skip_low = halves(skip[...] - skip_hi.astype(F32))
    skip_row = (
        dot(skip_hi, rep[0:GH, :]) + dot(skip_mid, rep[0:GH, :]) + dot(skip_low, rep[0:GH, :])
    )
    arrived(own, 24)
    pki[...] = jnp.transpose(own[...].astype(F32)).astype(BF)

    pl.semaphore_wait(barrier, NH + NC - 2)

    mine = block(me_h)

    def send_small(r, z):
        to = hpeer(r)
        remote(pki.at[heads(to), :], pkr.at[heads(me_h), :], 0, "head", to)
        return z

    lax.fori_loop(1, NH, send_small, 0)
    local(pki.at[heads(me_h), :], pkr.at[heads(me_h), :], 0)

    def send_maps(to):
        remote(bm, sm.at[0, mine, :], 1, "head", to)
        remote(cm, sm.at[1, mine, :], 1, "head", to)

    def send_maps_chip(r, z):
        send_maps(2 * lax.rem(chip + r, CHIPS) + core)
        return z

    lax.fori_loop(1, CHIPS, send_maps_chip, 0)
    send_maps(sibling)
    local(bm, sm.at[0, mine, :], 1)
    local(cm, sm.at[1, mine, :], 1)

    def send_wide(src, dst, s, h):
        def cols(k):
            return pl.ds(pl.multiple_of(k * W + h * HW, HW), HW)

        half = pl.ds(h * HW, HW)

        def one(r, z):
            to = hpeer(r)
            remote(src.at[:, cols(to)], dst.at[mine, half], s, "head", to)
            return z

        lax.fori_loop(1, NH, one, 0)
        local(src.at[:, cols(me_h)], dst.at[mine, half], s)

    send_wide(g, gb, 3, 0)
    send_wide(g, gb, 4, 1)
    send_wide(x, xb, 5, 0)
    send_wide(x, xb, 6, 1)

    arrived(pkr, 0)
    turned = jnp.transpose(pkr[...].astype(F32)).astype(BF)
    for k in range(NH):
        part = dot(turned, ones_where((row == k * GH + col) & (col < GH)))
        stc[k * TOK : (k + 1) * TOK, :] = part[0:TOK, :]
        cumc[k * TOK : (k + 1) * TOK, :] = part[TOK:, :]
    tots = []
    for c in range(CH):
        at = slice(c * Q, (c + 1) * Q)
        cum = dot(tri[...], cumc[at, :].astype(BF))
        cumc[at, :] = cum
        tots.append(cum[Q - 1 : Q, :])
    upto = [tots[0]]
    for c in range(1, CH):
        upto.append(upto[-1] + tots[c])
    beyond = [None] * CH
    beyond[CH - 1] = jnp.zeros_like(tots[0])
    for c in range(CH - 2, -1, -1):
        beyond[c] = beyond[c + 1] + tots[c + 1]
    for k in range(CH):
        prod[k : k + 1, 0:N] = tots[k]
        prod[CH + k : CH + k + 1, 0:N] = upto[k]
        prod[2 * CH + k : 2 * CH + k + 1, 0:N] = beyond[k]
        prod[3 * CH + k : 3 * CH + k + 1, 0:N] = jnp.zeros_like(tots[0])
    rows = jnp.exp(prod[:, 0:N])
    hi = rows.astype(BF)
    mid, low = halves(rows - hi.astype(F32))
    rowf[...] = dot(jnp.concatenate([hi, mid], axis=1), rep[...]) + dot(low, rep[0:N, :])
    for a in range(LG):
        for h in range(2):
            lanes = slice(h * HW + a * N, h * HW + (a + 1) * N)
            dec[a, h] = rowf[2 * CH - 1 : 2 * CH, lanes]

    def send_decay(r, z):
        k = cpeer(r)
        remote(dec.at[k // RG], decr.at[me_c], 7, "ctx", k)
        return z

    lax.fori_loop(1, NC, send_decay, 0)
    local(dec.at[me_c // RG], decr.at[me_c], 7)

    arrived(sm.at[:, pl.ds(0, 5 * TOK), :], 1)

    def pass_maps(r, z):
        at = block(2 * lax.rem(chip + r, CHIPS) + core)
        remote(sm.at[:, at, :], sm.at[:, at, :], 2, "head", sibling)
        return z

    lax.fori_loop(1, CHIPS, pass_maps, 0)

    def chunk(c):
        return pl.ds(pl.multiple_of(c * Q, Q), Q)

    def expand(a):
        return dot(jnp.concatenate(halves(a), axis=1), rep[...])

    for c in range(CH):
        at = slice(c * Q, (c + 1) * Q)
        cum = cumc[at, :]
        s = stc[at, :]
        f1[at, :] = expand(jnp.exp(cum))
        f2[at, :] = expand(s * jnp.exp(-cum))
        f1d[at, :] = expand(jnp.exp(cum + (upto[c] - tots[c])))
        f2d[at, :] = expand(s * jnp.exp(tots[c] - cum + beyond[c]))

    arrived(sm.at[:, pl.ds(0, 3 * TOK), :], 2)

    def transposed(a, out, c):
        t = jnp.transpose(a.astype(F32)).astype(BF)
        out[c, :, 0:Q] = t
        out[c, :, Q : 2 * Q] = t

    for c in range(CH):
        at = slice(c * Q, (c + 1) * Q)
        transposed(sm[0, at, :], bt2, c)
        transposed(sm[1, at, :], ct2, c)

    def stage(src, dst, h):
        for k in range(NC):
            a, b = k % RG * RB, h * HW + k // RG * N
            dst[h, k] = src[a : a + RB, b : b + N].astype(dst.dtype)

    def unstage(src, dst):
        for h in range(2):
            for k in range(NC):
                a, b = k % RG * RB, h * HW + k // RG * N
                dst[a : a + RB, b : b + N] = src[h, k].astype(dst.dtype)

    def spread(src, dst, s, h):
        def one(r, z):
            k = cpeer(r)
            remote(src.at[h, k], dst.at[h, me_c], s + h, "ctx", k)
            return z

        lax.fori_loop(1, NC, one, 0)
        local(src.at[h, me_c], dst.at[h, me_c], s + h)

    acc[...] = jnp.zeros_like(acc)
    for h in range(2):
        half = slice(h * HW, (h + 1) * HW)
        arrived(gb.at[:, pl.ds(h * HW, HW)], 3 + h)

        def step_g(r, z, half=half):
            c = CH - 1 - r
            at = chunk(c)
            ghi, glo = halves(gb[at, half].astype(F32) * f1[at, half])
            gx[c, 0:Q, half] = ghi
            end = acc[:, half]
            lg[c, :, half] = end
            end = end * rowf[pl.ds(c, 1), half]
            gx[c, Q : 2 * Q, half] = end.astype(BF)
            acc[:, half] = end + dot(ct2[c], jnp.concatenate([ghi, glo], axis=0))
            return z

        lax.fori_loop(0, CH, step_g, 0)
        stage(acc, gs, h)
        spread(gs, gr, 8, h)

    def step_u(c, z):
        at = chunk(c)
        b = sm[0, at, :]
        cb = jnp.where(above, dot(b, sm[1, at, :], NT), 0.0).astype(BF)
        v[at, :] = f2[at, :] * dot(jnp.concatenate([cb, b], axis=1), gx[c])
        return z

    lax.fori_loop(0, CH, step_u, 0)

    arrived(decr, 7)
    for h in range(2):
        arrived(gr.at[h], 8 + h)

        def back_g(r, carry, h=h):
            i = NC - 1 - r
            gbs[h, i] = carry.astype(BF)
            gf32[h, i] = carry
            return carry * decr[i, h] + gr[h, i].astype(F32)

        lax.fori_loop(0, NC, back_g, jnp.zeros((RB, N), F32))
        spread(gbs, gbr, 10, h)

    acc[...] = jnp.zeros_like(acc)
    for h in range(2):
        half = slice(h * HW, (h + 1) * HW)
        arrived(xb.at[:, pl.ds(h * HW, HW)], 5 + h)

        def step_x(c, z, half=half):
            at = chunk(c)
            xhi, xlo = halves(xb[at, half].astype(F32) * f2[at, half])
            xs[c, 0:Q, half] = xhi
            start = acc[:, half]
            ls[c, :, half] = start
            xs[c, Q : 2 * Q, half] = start.astype(BF)
            more = dot(bt2[c], jnp.concatenate([xhi, xlo], axis=0))
            acc[:, half] = (start + more) * rowf[pl.ds(c, 1), half]
            return z

        lax.fori_loop(0, CH, step_x, 0)
        ls[CH, :, half] = acc[:, half]
        stage(acc, ss, h)
        spread(ss, sr, 12, h)

    arrived(gbr.at[0], 10)
    arrived(gbr.at[1], 11)
    unstage(gbr, gin)

    def cols(k):
        return pl.ds(pl.multiple_of(k * W, W), W)

    def make_dx(p):
        at = chunk(p)
        now = v[at, :] + f2d[at, :] * dot(sm[0, at, :], gin[...])
        v[at, :] = now
        dxb[at, :] = (now + skip_row * gb[at, :].astype(F32)).astype(BF)

    def send_dx(to):
        remote(dxb.at[block(to), :], ox.at[:, cols(me_h)], 18, "head", to)

    def step_dx(r, z):
        p = lax.rem(chip + r, CHIPS)
        make_dx(p)
        send_dx(2 * p)
        send_dx(2 * p + 1)
        return z

    lax.fori_loop(1, CHIPS, step_dx, 0)
    make_dx(chip)
    send_dx(sibling)
    local(dxb.at[mine, :], ox.at[:, cols(me_h)], 18)

    for h in range(2):
        arrived(sr.at[h], 12 + h)

        def back_s(i, carry, h=h):
            sbs[h, i] = carry.astype(BF)
            pairs[h, i] = jnp.sum(carry * gf32[h, i], axis=0, keepdims=True)
            return carry * decr[i, h] + sr[h, i].astype(F32)

        lax.fori_loop(0, NC, back_s, jnp.zeros((RB, N), F32))
        spread(sbs, sbr, 14, h)
        spread(pairs, pairr, 16, h)

    def heads_sum(a):
        hi, lo = halves(a)
        return dot(hi, rep[0:N, :], NT) + dot(lo, rep[0:N, :], NT)

    def step_local(c, z):
        at = chunk(c)
        b, cc = sm[0, at, :], sm[1, at, :]
        gh, xh = gx[c, 0:Q, :], xs[c, 0:Q, :]
        xf, gf = xb[at, :].astype(F32), gb[at, :].astype(F32)
        cs[at, :] = heads_sum(xf * v[at, :])
        e = jnp.where(below, dot(gh, xh, NT), 0.0).astype(BF)
        et = jnp.where(above, dot(xh, gh, NT), 0.0).astype(BF)
        gk = (
            dot(et, cc)
            + dot(xh, gx[c, Q : 2 * Q, :], NT)
            + dot((xf * f2d[at, :]).astype(BF), gin[...], NT)
        )
        gq = dot(e, b) + dot(gh, xs[c, Q : 2 * Q, :], NT)
        for k in range(2):
            gbp[c, k] = gk[k * TOK : (k + 1) * TOK, :]
            gcp[c, k] = gq[k * TOK : (k + 1) * TOK, :]
        cb = jnp.where(below, dot(cc, b, NT), 0.0).astype(BF)
        y = f1[at, :] * dot(jnp.concatenate([cb, cc], axis=1), xs[c])
        rs[at, :] = heads_sum(gf * y)
        return z

    lax.fori_loop(0, CH, step_local, 0)

    def share(src, dst, s):
        remote(src.at[:, 1 - core], dst, s, "head", sibling)

    def share_far(src, dst, near, out, s, s2):
        arrived(dst, s)
        near[...] = src[:, pl.ds(core, 1)].reshape(CHIPS, TOK, N) + dst[...]

        def one(r, z):
            p = lax.rem(chip + r, CHIPS)
            remote(near.at[p], out.at[chip], s2, "head", 2 * p + core)
            return z

        lax.fori_loop(1, CHIPS, one, 0)
        local(near.at[chip], out.at[chip], s2)

    share(gbp, gbo, 19)

    arrived(sbr.at[0], 14)
    arrived(sbr.at[1], 15)
    unstage(sbr, sin)
    share_far(gbp, gbo, gbh, gbrv, 19, 20)

    def step_s(c, z):
        at = chunk(c)
        gf = gb[at, :].astype(F32)
        gd = gf * f1d[at, :]
        gq = dot(gd.astype(BF), sin[...], NT)
        for k in range(2):
            gcp[c, k] = gcp[c, k] + gq[k * TOK : (k + 1) * TOK, :]
        rs[at, :] = rs[at, :] + heads_sum(gd * dot(sm[1, at, :], sin[...]))
        return z

    lax.fori_loop(0, CH, step_s, 0)
    share(gcp, gco, 21)

    arrived(pairr.at[0], 16)
    arrived(pairr.at[1], 17)
    gi, si = gin[...].astype(F32), sin[...].astype(F32)
    exact = []
    for h in range(2):
        for a in range(LG):
            exact.append(jnp.sum(pairr[h, a * RG : (a + 1) * RG], axis=0))
    fix = rowf[2 * CH - 1 : 2 * CH, :] * (
        jnp.concatenate(exact, axis=1) - jnp.sum(gi * si, axis=0, keepdims=True)
    )
    prod[...] = jnp.zeros_like(prod)
    for c in range(CH):
        ge = lg[c] + rowf[2 * CH + c : 2 * CH + c + 1, :] * gi
        se = ls[c + 1] + rowf[CH + c : CH + c + 1, :] * si
        prod[c : c + 1, :] = jnp.sum(ge * se, axis=0, keepdims=True) + fix
    base = heads_sum(prod[...])
    lane = iota((Q, N), 1)
    upper = ones_where(above)
    packed = jnp.zeros((2 * TOK, N), F32)
    for c in range(CH):
        at = slice(c * Q, (c + 1) * Q)
        csum = cs[at, :]
        hi, lo = halves(rs[at, :] - csum)
        dq = base[c : c + 1, :] + dot(upper, hi) + dot(upper, lo)
        ds = jnp.where(lane < GH, csum / jnp.where(lane < GH, stc[at, :], 1.0), 0.0)
        for k in range(2):
            half = slice(k * TOK, (k + 1) * TOK)
            both = jnp.concatenate([ds[half, :], dq[half, :]], axis=0)
            turn = (2 * c + k) * GH
            packed = packed + (pltpu.roll(both, turn, 1) if turn else both)
    pko[...] = jnp.transpose(packed).astype(BF)

    def send_pk(r, z):
        to = hpeer(r)
        remote(pko.at[heads(to), :], pkv.at[heads(me_h), :], 23, "head", to)
        return z

    lax.fori_loop(1, NH, send_pk, 0)
    local(pko.at[heads(me_h), :], pkv.at[heads(me_h), :], 23)

    share_far(gcp, gco, gch, gcrv, 21, 22)

    arrived(gbrv, 20)
    ogb[...] = jnp.sum(gbrv[...], axis=0)
    arrived(pkv, 23)
    back = jnp.transpose(pkv[...].astype(F32)).astype(BF)
    ods[...] = back[0:TOK, :]
    odq[...] = back[TOK:, :]
    arrived(gcrv, 22)
    ogc[...] = jnp.sum(gcrv[...], axis=0)
    arrived(ox, 18)

    left(pkr.at[pl.ds(0, N - GH), :], 0)
    left(sm.at[:, pl.ds(0, 4 * TOK), :], 1)
    left(sm.at[:, pl.ds(0, 3 * TOK), :], 2)
    for h in range(2):
        left(gb.at[pl.ds(0, LEN - TOK), pl.ds(0, HW)], 3 + h)
        left(xb.at[pl.ds(0, LEN - TOK), pl.ds(0, HW)], 5 + h)
        left(gs.at[h, pl.ds(0, NC - 1)], 8 + h)
        left(gbs.at[h, pl.ds(0, NC - 1)], 10 + h)
        left(ss.at[h, pl.ds(0, NC - 1)], 12 + h)
        left(sbs.at[h, pl.ds(0, NC - 1)], 14 + h)
        left(pairs.at[h, pl.ds(0, NC - 1)], 16 + h)
    left(decr.at[pl.ds(0, NC - 1)], 7)
    left(dxb.at[pl.ds(0, LEN - TOK), :], 18)
    left(gbo, 19)
    left(gbh.at[pl.ds(0, CHIPS - 1)], 20)
    left(gco, 21)
    left(gch.at[pl.ds(0, CHIPS - 1)], 22)
    left(pkv.at[pl.ds(0, N - GH), :], 23)


def body(inputs, grad_out, steps, log_decay, input_map, output_map, skip_gain):
    hbm = pl.BlockSpec(memory_space=pl.ANY)
    vmem = pl.BlockSpec(memory_space=pltpu.VMEM)

    def vm(shape, kind):
        return pltpu.VMEM(shape, kind)

    grads = pl.pallas_call(
        kernel,
        out_shape=(
            jax.ShapeDtypeStruct((TOK, NH * W), BF),
            jax.ShapeDtypeStruct((TOK, N), BF),
            jax.ShapeDtypeStruct((TOK, N), BF),
            jax.ShapeDtypeStruct((TOK, N), F32),
            jax.ShapeDtypeStruct((TOK, N), F32),
        ),
        in_specs=[hbm] * 6 + [vmem],
        out_specs=(hbm, vmem, vmem, vmem, vmem),
        scratch_shapes=[
            vm((LEN, W), BF),
            vm((LEN, W), BF),
            vm((2, LEN, N), BF),
            vm((2 * TOK, N), BF),
            vm((N, 2 * TOK), BF),
            vm((N, 2 * TOK), BF),
            vm((2 * N, W), BF),
            vm((LEN, W), F32),
            vm((LEN, W), F32),
            vm((LEN, W), F32),
            vm((LEN, W), F32),
            vm((4 * CH, W), F32),
            vm((Q, Q), BF),
            vm((LEN, N), F32),
            vm((LEN, N), F32),
            vm((CH, N, 2 * Q), BF),
            vm((CH, N, 2 * Q), BF),
            vm((CH, 2 * Q, W), BF),
            vm((CH, 2 * Q, W), BF),
            vm((CH, N, W), F32),
            vm((CH + 1, N, W), F32),
            vm((N, W), F32),
            vm((LEN, W), F32),
            vm((LEN, W), BF),
            vm((N, W), BF),
            vm((N, W), BF),
            vm((LG, 2, 1, N), F32),
            vm((NC, 2, 1, N), F32),
            vm((2, NC, RB, N), BF),
            vm((2, NC, RB, N), BF),
            vm((2, NC, RB, N), BF),
            vm((2, NC, RB, N), BF),
            vm((2, NC, RB, N), F32),
            vm((2, NC, RB, N), BF),
            vm((2, NC, RB, N), BF),
            vm((2, NC, RB, N), BF),
            vm((2, NC, RB, N), BF),
            vm((2, NC, 1, N), F32),
            vm((2, NC, 1, N), F32),
            vm((LEN, N), F32),
            vm((LEN, N), F32),
            vm((4 * CH, W), F32),
            vm((CHIPS, 2, TOK, N), F32),
            vm((CHIPS, 2, TOK, N), F32),
            vm((CHIPS, TOK, N), F32),
            vm((CHIPS, TOK, N), F32),
            vm((CHIPS, TOK, N), F32),
            vm((CHIPS, TOK, N), F32),
            vm((CHIPS, TOK, N), F32),
            vm((CHIPS, TOK, N), F32),
            vm((N, 2 * TOK), BF),
            vm((N, 2 * TOK), BF),
            pltpu.SemaphoreType.DMA((24,)),
            pltpu.SemaphoreType.DMA((25,)),
        ],
        compiler_params=pltpu.CompilerParams(
            collective_id=0, has_side_effects=True, vmem_limit_bytes=56 * 1024 * 1024
        ),
        cost_estimate=pl.CostEstimate(
            flops=3 * 10**9, bytes_accessed=8 * 2**20, transcendentals=2**20
        ),
        name="block_backward",
    )(inputs, grad_out, steps, log_decay, input_map, output_map, skip_gain.reshape(1, GH))
    return grads


def solution(mesh):
    spread = P(("ctx", "head"), None)
    return jax.shard_map(
        body,
        mesh=mesh,
        in_specs=(spread,) * 6 + (P("head"),),
        out_specs=(spread,) * 5,
        check_vma=False,
    )
```

```python
import jax
import jax.numpy as jnp
from jax import lax
from jax.experimental import pallas as pl
from jax.experimental.pallas import tpu as pltpu
from jax.sharding import PartitionSpec as P

BF = jnp.bfloat16
F32 = jnp.float32
MESH = pl.DeviceIdType.MESH
NC = 32
NH = 8
TOK = 64
LEN = 512
Q = 128
CH = LEN // Q
W = 1024
HD = 64
N = 128
GH = 16
HW = W // 2
RB = 16
RG = N // RB
LG = HW // N
CHIPS = NH // 2

NN = ((1,), (0,))
NT = ((1,), (1,))


def dot(a, b, dims=NN):
    return lax.dot_general(a, b, (dims, ((), ())), preferred_element_type=F32)


def halves(a):
    hi = a.astype(BF)
    return hi, (a - hi.astype(F32)).astype(BF)


def iota(shape, axis):
    return lax.broadcasted_iota(jnp.int32, shape, axis)


def ones_where(cond):
    return jnp.where(cond, 1.0, 0.0).astype(BF)


def kernel(
    x, g, st, ld, bm, cm, skip, ox, pkv, gbrv, gcrv,
    gb, xb, sm, own, pki, pkr, rep, f1, f2, f1d, f2d, rowf, tri, stc, cumc, ct2, bt2, gx, xs,
    lg, ls, acc, v, dxb, gin, sin, dec, decr, gs, gr, gbs, gbr, gf32, ss, sr, sbs, sbr, pairs, pairr,
    cs, rs, prod, gbp, gcp, gbo, gbh, gcb, pko, send, recv,
):
    me_c = lax.axis_index("ctx")
    me_h = lax.axis_index("head")
    core = lax.rem(me_h, 2)
    chip = me_h // 2
    sibling = me_h + 1 - 2 * core

    def cpeer(r):
        return lax.rem(me_c + r, NC)

    def hpeer(r):
        return lax.rem(me_h + r, NH)

    def remote(src, dst, s, axis, to):
        pltpu.make_async_remote_copy(
            src_ref=src, dst_ref=dst, send_sem=send.at[s], recv_sem=recv.at[s],
            device_id={axis: to}, device_id_type=MESH,
        ).start()

    def local(src, dst, s):
        pltpu.make_async_copy(src, dst, recv.at[s]).start()

    def arrived(ref, s):
        pltpu.make_async_copy(ref, ref, recv.at[s]).wait()

    def left(ref, s):
        pltpu.make_async_copy(ref, ref, send.at[s]).wait()

    def block(k):
        return pl.ds(pl.multiple_of(k * TOK, TOK), TOK)

    def heads(k):
        return pl.ds(pl.multiple_of(k * GH, GH), GH)

    barrier = pltpu.get_barrier_semaphore()

    def greet_head(r, z):
        pl.semaphore_signal(barrier, inc=1, device_id={"head": hpeer(r)}, device_id_type=MESH)
        return z

    def greet_ctx(r, z):
        pl.semaphore_signal(barrier, inc=1, device_id={"ctx": cpeer(r)}, device_id_type=MESH)
        return z

    lax.fori_loop(1, NH, greet_head, 0)
    lax.fori_loop(1, NC, greet_ctx, 0)

    local(st, own.at[pl.ds(0, TOK), :], 24)
    local(ld, own.at[pl.ds(TOK, TOK), :], 24)
    rep_one = ones_where(iota((N, W), 0) == iota((N, W), 1) // HD)
    rep[0:N, :] = rep_one
    rep[N : 2 * N, :] = rep_one
    row, col = iota((Q, Q), 0), iota((Q, Q), 1)
    tri[...] = ones_where(row >= col)
    below = row >= col
    above = row <= col
    skip_hi = skip[...].astype(BF)
    skip_mid, skip_low = halves(skip[...] - skip_hi.astype(F32))
    skip_row = (
        dot(skip_hi, rep[0:GH, :]) + dot(skip_mid, rep[0:GH, :]) + dot(skip_low, rep[0:GH, :])
    )
    arrived(own, 24)
    pki[...] = jnp.transpose(own[...].astype(F32)).astype(BF)

    pl.semaphore_wait(barrier, NH + NC - 2)

    mine = block(me_h)

    def send_small(r, z):
        to = hpeer(r)
        remote(pki.at[heads(to), :], pkr.at[heads(me_h), :], 0, "head", to)
        return z

    lax.fori_loop(1, NH, send_small, 0)
    local(pki.at[heads(me_h), :], pkr.at[heads(me_h), :], 0)

    def send_maps(to):
        remote(bm, sm.at[0, mine, :], 1, "head", to)
        remote(cm, sm.at[1, mine, :], 1, "head", to)

    def send_maps_chip(r, z):
        send_maps(2 * lax.rem(chip + r, CHIPS) + core)
        return z

    lax.fori_loop(1, CHIPS, send_maps_chip, 0)
    send_maps(sibling)
    local(bm, sm.at[0, mine, :], 1)
    local(cm, sm.at[1, mine, :], 1)

    def send_wide(src, dst, s, h):
        def cols(k):
            return pl.ds(pl.multiple_of(k * W + h * HW, HW), HW)

        half = pl.ds(h * HW, HW)

        def one(r, z):
            to = hpeer(r)
            remote(src.at[:, cols(to)], dst.at[mine, half], s, "head", to)
            return z

        lax.fori_loop(1, NH, one, 0)
        local(src.at[:, cols(me_h)], dst.at[mine, half], s)

    send_wide(g, gb, 3, 0)
    send_wide(g, gb, 4, 1)
    send_wide(x, xb, 5, 0)
    send_wide(x, xb, 6, 1)

    arrived(pkr, 0)
    turned = jnp.transpose(pkr[...].astype(F32)).astype(BF)
    for k in range(NH):
        part = dot(turned, ones_where((row == k * GH + col) & (col < GH)))
        stc[k * TOK : (k + 1) * TOK, :] = part[0:TOK, :]
        cumc[k * TOK : (k + 1) * TOK, :] = part[TOK:, :]
    tots = []
    for c in range(CH):
        at = slice(c * Q, (c + 1) * Q)
        cum = dot(tri[...], cumc[at, :].astype(BF))
        cumc[at, :] = cum
        tots.append(cum[Q - 1 : Q, :])
    upto = [tots[0]]
    for c in range(1, CH):
        upto.append(upto[-1] + tots[c])
    beyond = [None] * CH
    beyond[CH - 1] = jnp.zeros_like(tots[0])
    for c in range(CH - 2, -1, -1):
        beyond[c] = beyond[c + 1] + tots[c + 1]
    for k in range(CH):
        prod[k : k + 1, 0:N] = tots[k]
        prod[CH + k : CH + k + 1, 0:N] = upto[k]
        prod[2 * CH + k : 2 * CH + k + 1, 0:N] = beyond[k]
        prod[3 * CH + k : 3 * CH + k + 1, 0:N] = jnp.zeros_like(tots[0])
    rows = jnp.exp(prod[:, 0:N])
    hi = rows.astype(BF)
    mid, low = halves(rows - hi.astype(F32))
    rowf[...] = dot(jnp.concatenate([hi, mid], axis=1), rep[...]) + dot(low, rep[0:N, :])
    for a in range(LG):
        for h in range(2):
            lanes = slice(h * HW + a * N, h * HW + (a + 1) * N)
            dec[a, h] = rowf[2 * CH - 1 : 2 * CH, lanes]

    def send_decay(r, z):
        k = cpeer(r)
        remote(dec.at[k // RG], decr.at[me_c], 7, "ctx", k)
        return z

    lax.fori_loop(1, NC, send_decay, 0)
    local(dec.at[me_c // RG], decr.at[me_c], 7)

    arrived(sm.at[:, pl.ds(0, 5 * TOK), :], 1)

    def pass_maps(r, z):
        at = block(2 * lax.rem(chip + r, CHIPS) + core)
        remote(sm.at[:, at, :], sm.at[:, at, :], 2, "head", sibling)
        return z

    lax.fori_loop(1, CHIPS, pass_maps, 0)

    def chunk(c):
        return pl.ds(pl.multiple_of(c * Q, Q), Q)

    def expand(a):
        return dot(jnp.concatenate(halves(a), axis=1), rep[...])

    for c in range(CH):
        at = slice(c * Q, (c + 1) * Q)
        cum = cumc[at, :]
        s = stc[at, :]
        f1[at, :] = expand(jnp.exp(cum))
        f2[at, :] = expand(s * jnp.exp(-cum))
        f1d[at, :] = expand(jnp.exp(cum + (upto[c] - tots[c])))
        f2d[at, :] = expand(s * jnp.exp(tots[c] - cum + beyond[c]))

    arrived(sm.at[:, pl.ds(0, 3 * TOK), :], 2)

    def transposed(a, out, c):
        t = jnp.transpose(a.astype(F32)).astype(BF)
        out[c, :, 0:Q] = t
        out[c, :, Q : 2 * Q] = t

    for c in range(CH):
        at = slice(c * Q, (c + 1) * Q)
        transposed(sm[0, at, :], bt2, c)
        transposed(sm[1, at, :], ct2, c)

    def stage(src, dst, h):
        for k in range(NC):
            a, b = k % RG * RB, h * HW + k // RG * N
            dst[h, k] = src[a : a + RB, b : b + N].astype(dst.dtype)

    def unstage(src, dst, h):
        for k in range(NC):
            a, b = k % RG * RB, h * HW + k // RG * N
            dst[a : a + RB, b : b + N] = src[h, k]

    def spread(src, dst, s, h):
        def one(r, z):
            k = cpeer(r)
            remote(src.at[h, k], dst.at[h, me_c], s + h, "ctx", k)
            return z

        lax.fori_loop(1, NC, one, 0)
        local(src.at[h, me_c], dst.at[h, me_c], s + h)

    def half_of(h):
        return slice(h * HW, (h + 1) * HW)

    def local_u(h):
        half = half_of(h)

        def step_u(c, z):
            at = chunk(c)
            b = sm[0, at, :]
            cb = jnp.where(above, dot(b, sm[1, at, :], NT), 0.0).astype(BF)
            v[at, half] = f2[at, half] * dot(jnp.concatenate([cb, b], axis=1), gx[c, :, half])
            return z

        lax.fori_loop(0, CH, step_u, 0)

    def owners_g(h):
        arrived(gr.at[h], 8 + h)

        def back_g(r, carry):
            i = NC - 1 - r
            gbs[h, i] = carry.astype(BF)
            gf32[h, i] = carry
            return carry * decr[i, h] + gr[h, i].astype(F32)

        lax.fori_loop(0, NC, back_g, jnp.zeros((RB, N), F32))
        spread(gbs, gbr, 10, h)

    def local_g(h):
        half = half_of(h)
        arrived(gb.at[:, pl.ds(h * HW, HW)], 3 + h)
        acc[:, half] = jnp.zeros((N, HW), F32)

        def step_g(r, z):
            c = CH - 1 - r
            at = chunk(c)
            ghi, glo = halves(gb[at, half].astype(F32) * f1[at, half])
            gx[c, 0:Q, half] = ghi
            end = acc[:, half]
            lg[c, :, half] = end
            end = end * rowf[pl.ds(c, 1), half]
            gx[c, Q : 2 * Q, half] = end.astype(BF)
            acc[:, half] = end + dot(ct2[c], jnp.concatenate([ghi, glo], axis=0))
            return z

        lax.fori_loop(0, CH, step_g, 0)
        stage(acc, gs, h)
        spread(gs, gr, 8, h)

    def local_x(h):
        half = half_of(h)
        arrived(xb.at[:, pl.ds(h * HW, HW)], 5 + h)
        acc[:, half] = jnp.zeros((N, HW), F32)

        def step_x(c, z):
            at = chunk(c)
            xhi, xlo = halves(xb[at, half].astype(F32) * f2[at, half])
            xs[c, 0:Q, half] = xhi
            start = acc[:, half]
            ls[c, :, half] = start
            xs[c, Q : 2 * Q, half] = start.astype(BF)
            more = dot(bt2[c], jnp.concatenate([xhi, xlo], axis=0))
            acc[:, half] = (start + more) * rowf[pl.ds(c, 1), half]
            return z

        lax.fori_loop(0, CH, step_x, 0)
        ls[CH, :, half] = acc[:, half]
        stage(acc, ss, h)
        spread(ss, sr, 12, h)

    def channels(h):
        half = half_of(h)
        arrived(gbr.at[h], 10 + h)
        unstage(gbr, gin, h)
        there = pl.ds(pl.multiple_of(me_h * W + h * HW, HW), HW)

        def make_dx(p):
            at = chunk(p)
            now = v[at, half] + f2d[at, half] * dot(sm[0, at, :], gin[:, half])
            v[at, half] = now
            dxb[at, half] = (now + skip_row[:, half] * gb[at, half].astype(F32)).astype(BF)

        def send_dx(to):
            remote(dxb.at[block(to), pl.ds(h * HW, HW)], ox.at[:, there], 18, "head", to)

        def step_dx(r, z):
            p = lax.rem(chip + r, CHIPS)
            make_dx(p)
            send_dx(2 * p)
            send_dx(2 * p + 1)
            return z

        lax.fori_loop(1, CHIPS, step_dx, 0)
        make_dx(chip)
        send_dx(sibling)
        local(dxb.at[mine, pl.ds(h * HW, HW)], ox.at[:, there], 18)

    def owners_s(h):
        arrived(sr.at[h], 12 + h)

        def back_s(i, carry):
            sbs[h, i] = carry.astype(BF)
            pairs[i, h] = jnp.sum(carry * gf32[h, i], axis=0, keepdims=True)
            return carry * decr[i, h] + sr[h, i].astype(F32)

        lax.fori_loop(0, NC, back_s, jnp.zeros((RB, N), F32))
        spread(sbs, sbr, 14, h)

    local_g(0)
    local_u(0)
    local_g(1)
    arrived(decr, 7)
    owners_g(0)
    local_u(1)
    owners_g(1)
    local_x(0)
    channels(0)
    local_x(1)
    channels(1)
    owners_s(0)
    owners_s(1)

    def send_pairs(r, z):
        k = cpeer(r)
        remote(pairs.at[k], pairr.at[me_c], 16, "ctx", k)
        return z

    lax.fori_loop(1, NC, send_pairs, 0)
    local(pairs.at[me_c], pairr.at[me_c], 16)

    def heads_sum(a, half=slice(0, W)):
        hi, lo = halves(a)
        return dot(hi, rep[0:N, half], NT) + dot(lo, rep[0:N, half], NT)

    def step_local(c, z):
        at = chunk(c)
        b, cc = sm[0, at, :], sm[1, at, :]
        gh, xh = gx[c, 0:Q, :], xs[c, 0:Q, :]
        xf, gf = xb[at, :].astype(F32), gb[at, :].astype(F32)
        cs[at, :] = heads_sum(xf * v[at, :])
        e = jnp.where(below, dot(gh, xh, NT), 0.0).astype(BF)
        et = jnp.where(above, dot(xh, gh, NT), 0.0).astype(BF)
        gk = (
            dot(et, cc)
            + dot(xh, gx[c, Q : 2 * Q, :], NT)
            + dot((xf * f2d[at, :]).astype(BF), gin[...], NT)
        )
        gq = dot(e, b) + dot(gh, xs[c, Q : 2 * Q, :], NT)
        for k in range(2):
            gbp[c, k] = gk[k * TOK : (k + 1) * TOK, :]
            gcp[c, k] = gq[k * TOK : (k + 1) * TOK, :]
        cb = jnp.where(below, dot(cc, b, NT), 0.0).astype(BF)
        y = f1[at, :] * dot(jnp.concatenate([cb, cc], axis=1), xs[c])
        rs[at, :] = heads_sum(gf * y)
        return z

    lax.fori_loop(0, CH, step_local, 0)
    remote(gbp.at[:, 1 - core], gbo, 19, "head", sibling)

    def use_s(h):
        half = half_of(h)
        arrived(sbr.at[h], 14 + h)
        unstage(sbr, sin, h)

        def step_s(c, z):
            at = chunk(c)
            gd = gb[at, half].astype(F32) * f1d[at, half]
            gq = dot(gd.astype(BF), sin[:, half], NT)
            for k in range(2):
                now = gcp[c, k] + gq[k * TOK : (k + 1) * TOK, :]
                if h == 0:
                    gcp[c, k] = now
                else:
                    gcb[c, k] = now.astype(BF)
            rs[at, :] = rs[at, :] + heads_sum(gd * dot(sm[1, at, :], sin[:, half]), half)
            return z

        lax.fori_loop(0, CH, step_s, 0)

    use_s(0)
    arrived(gbo, 19)
    gbh[...] = gbp[:, pl.ds(core, 1)].reshape(CHIPS, TOK, N) + gbo[...]

    def send_gb(r, z):
        p = lax.rem(chip + r, CHIPS)
        remote(gbh.at[p], gbrv.at[chip], 20, "head", 2 * p + core)
        return z

    lax.fori_loop(1, CHIPS, send_gb, 0)
    local(gbh.at[chip], gbrv.at[chip], 20)

    use_s(1)

    def send_gc(r, z):
        to = hpeer(r)
        remote(gcb.at[to // 2, lax.rem(to, 2)], gcrv.at[me_h], 21, "head", to)
        return z

    lax.fori_loop(1, NH, send_gc, 0)
    local(gcb.at[chip, core], gcrv.at[me_h], 21)

    arrived(pairr, 16)
    gi, si = gin[...].astype(F32), sin[...].astype(F32)
    exact = []
    for h in range(2):
        for a in range(LG):
            exact.append(jnp.sum(pairr[a * RG : (a + 1) * RG, h], axis=0))
    fix = rowf[2 * CH - 1 : 2 * CH, :] * (
        jnp.concatenate(exact, axis=1) - jnp.sum(gi * si, axis=0, keepdims=True)
    )
    prod[...] = jnp.zeros_like(prod)
    for c in range(CH):
        ge = lg[c] + rowf[2 * CH + c : 2 * CH + c + 1, :] * gi
        se = ls[c + 1] + rowf[CH + c : CH + c + 1, :] * si
        prod[c : c + 1, :] = jnp.sum(ge * se, axis=0, keepdims=True) + fix
    base = heads_sum(prod[...])
    lane = iota((Q, N), 1)
    upper = ones_where(above)
    packed = jnp.zeros((2 * TOK, N), F32)
    for c in range(CH):
        at = slice(c * Q, (c + 1) * Q)
        csum = cs[at, :]
        hi, lo = halves(rs[at, :] - csum)
        dq = base[c : c + 1, :] + dot(upper, hi) + dot(upper, lo)
        ds = jnp.where(lane < GH, csum / jnp.where(lane < GH, stc[at, :], 1.0), 0.0)
        for k in range(2):
            half = slice(k * TOK, (k + 1) * TOK)
            both = jnp.concatenate([ds[half, :], dq[half, :]], axis=0)
            turn = (2 * c + k) * GH
            packed = packed + (pltpu.roll(both, turn, 1) if turn else both)
    pko[...] = jnp.transpose(packed).astype(BF)

    def send_pk(r, z):
        to = hpeer(r)
        remote(pko.at[heads(to), :], pkv.at[heads(me_h), :], 23, "head", to)
        return z

    lax.fori_loop(1, NH, send_pk, 0)
    local(pko.at[heads(me_h), :], pkv.at[heads(me_h), :], 23)

    arrived(gbrv, 20)
    arrived(pkv, 23)
    arrived(gcrv, 21)
    arrived(ox, 18)

    left(pkr.at[pl.ds(0, N - GH), :], 0)
    left(sm.at[:, pl.ds(0, 4 * TOK), :], 1)
    left(sm.at[:, pl.ds(0, 3 * TOK), :], 2)
    for h in range(2):
        left(gb.at[pl.ds(0, LEN - TOK), pl.ds(0, HW)], 3 + h)
        left(xb.at[pl.ds(0, LEN - TOK), pl.ds(0, HW)], 5 + h)
        left(gs.at[h, pl.ds(0, NC - 1)], 8 + h)
        left(gbs.at[h, pl.ds(0, NC - 1)], 10 + h)
        left(ss.at[h, pl.ds(0, NC - 1)], 12 + h)
        left(sbs.at[h, pl.ds(0, NC - 1)], 14 + h)
    left(decr.at[pl.ds(0, NC - 1)], 7)
    left(pairr.at[pl.ds(0, NC - 1)], 16)
    left(dxb.at[pl.ds(0, LEN - TOK), :], 18)
    left(gbo, 19)
    left(gbh.at[pl.ds(0, CHIPS - 1)], 20)
    left(gcrv.at[pl.ds(0, NH - 1)], 21)
    left(pkv.at[pl.ds(0, N - GH), :], 23)


def finish(ox, pkv, gbrv, gcrv, odx, ods, odq, ogb, ogc, sem):
    move = pltpu.make_async_copy(ox, odx, sem)
    move.start()
    back = jnp.transpose(pkv[...].astype(F32)).astype(BF)
    ods[...] = back[0:TOK, :]
    odq[...] = back[TOK:, :]
    ogb[...] = jnp.sum(gbrv[...], axis=0)
    ogc[...] = jnp.sum(gcrv[...].astype(F32), axis=0)
    move.wait()


def body(inputs, grad_out, steps, log_decay, input_map, output_map, skip_gain):
    hbm = pl.BlockSpec(memory_space=pl.ANY)
    vmem = pl.BlockSpec(memory_space=pltpu.VMEM)

    def vm(shape, kind):
        return pltpu.VMEM(shape, kind)

    parts = pl.pallas_call(
        kernel,
        out_shape=(
            jax.ShapeDtypeStruct((TOK, NH * W), BF),
            jax.ShapeDtypeStruct((N, 2 * TOK), BF),
            jax.ShapeDtypeStruct((CHIPS, TOK, N), F32),
            jax.ShapeDtypeStruct((NH, TOK, N), BF),
        ),
        in_specs=[hbm] * 6 + [vmem],
        out_specs=(hbm,) * 4,
        scratch_shapes=[
            vm((LEN, W), BF),
            vm((LEN, W), BF),
            vm((2, LEN, N), BF),
            vm((2 * TOK, N), BF),
            vm((N, 2 * TOK), BF),
            vm((N, 2 * TOK), BF),
            vm((2 * N, W), BF),
            vm((LEN, W), F32),
            vm((LEN, W), F32),
            vm((LEN, W), F32),
            vm((LEN, W), F32),
            vm((4 * CH, W), F32),
            vm((Q, Q), BF),
            vm((LEN, N), F32),
            vm((LEN, N), F32),
            vm((CH, N, 2 * Q), BF),
            vm((CH, N, 2 * Q), BF),
            vm((CH, 2 * Q, W), BF),
            vm((CH, 2 * Q, W), BF),
            vm((CH, N, W), F32),
            vm((CH + 1, N, W), F32),
            vm((N, W), F32),
            vm((LEN, W), F32),
            vm((LEN, W), BF),
            vm((N, W), BF),
            vm((N, W), BF),
            vm((LG, 2, 1, N), F32),
            vm((NC, 2, 1, N), F32),
            vm((2, NC, RB, N), BF),
            vm((2, NC, RB, N), BF),
            vm((2, NC, RB, N), BF),
            vm((2, NC, RB, N), BF),
            vm((2, NC, RB, N), F32),
            vm((2, NC, RB, N), BF),
            vm((2, NC, RB, N), BF),
            vm((2, NC, RB, N), BF),
            vm((2, NC, RB, N), BF),
            vm((NC, 2, 1, N), F32),
            vm((NC, 2, 1, N), F32),
            vm((LEN, N), F32),
            vm((LEN, N), F32),
            vm((4 * CH, W), F32),
            vm((CHIPS, 2, TOK, N), F32),
            vm((CHIPS, 2, TOK, N), F32),
            vm((CHIPS, TOK, N), F32),
            vm((CHIPS, TOK, N), F32),
            vm((CHIPS, 2, TOK, N), BF),
            vm((N, 2 * TOK), BF),
            pltpu.SemaphoreType.DMA((24,)),
            pltpu.SemaphoreType.DMA((25,)),
        ],
        compiler_params=pltpu.CompilerParams(
            collective_id=0, has_side_effects=True, vmem_limit_bytes=56 * 1024 * 1024
        ),
        cost_estimate=pl.CostEstimate(
            flops=3 * 10**9, bytes_accessed=8 * 2**20, transcendentals=2**20
        ),
        name="block_backward",
    )(inputs, grad_out, steps, log_decay, input_map, output_map, skip_gain.reshape(1, GH))
    return pl.pallas_call(
        finish,
        out_shape=(
            jax.ShapeDtypeStruct((TOK, NH * W), BF),
            jax.ShapeDtypeStruct((TOK, N), BF),
            jax.ShapeDtypeStruct((TOK, N), BF),
            jax.ShapeDtypeStruct((TOK, N), F32),
            jax.ShapeDtypeStruct((TOK, N), F32),
        ),
        in_specs=[hbm, vmem, vmem, vmem],
        out_specs=(hbm, vmem, vmem, vmem, vmem),
        scratch_shapes=[pltpu.SemaphoreType.DMA],
        cost_estimate=pl.CostEstimate(flops=2**20, bytes_accessed=3 * 2**20, transcendentals=0),
        name="finish",
    )(*parts)


def solution(mesh):
    spread = P(("ctx", "head"), None)
    return jax.shard_map(
        body,
        mesh=mesh,
        in_specs=(spread,) * 6 + (P("head"),),
        out_specs=(spread,) * 5,
        check_vma=False,
    )
```

```python
import jax
import jax.numpy as jnp
from jax import lax
from jax.experimental import pallas as pl
from jax.experimental.pallas import tpu as pltpu
from jax.sharding import PartitionSpec as P

BF = jnp.bfloat16
F32 = jnp.float32
MESH = pl.DeviceIdType.MESH
NC = 32
NH = 8
TOK = 64
LEN = 512
Q = 128
CH = LEN // Q
W = 1024
HD = 64
N = 128
GH = 16
HW = W // 2
RB = 16
RG = N // RB
LG = HW // N
CHIPS = NH // 2

NN = ((1,), (0,))
NT = ((1,), (1,))


def dot(a, b, dims=NN):
    return lax.dot_general(a, b, (dims, ((), ())), preferred_element_type=F32)


def halves(a):
    hi = a.astype(BF)
    return hi, (a - hi.astype(F32)).astype(BF)


def iota(shape, axis):
    return lax.broadcasted_iota(jnp.int32, shape, axis)


def ones_where(cond):
    return jnp.where(cond, 1.0, 0.0).astype(BF)


def kernel(
    x, g, st, ld, bm, cm, skip, ox, pkv, gbrv, gcrv,
    gb, xb, sm, own, pki, pkr, rep, f1, f2, f1d, f2d, rowf, tri, stc, cumc, ct2, bt2, gx, xs,
    lg, ls, acc, v, dxb, gin, sin, dec, decr, gs, gr, gbs, gbr, gf32, ss, sr, sbs, sbr, pairs, pairr,
    cs, rs, prod, gbp, gcp, gbo, gbh, gcb, pko, send, recv,
):
    me_c = lax.axis_index("ctx")
    me_h = lax.axis_index("head")
    core = lax.rem(me_h, 2)
    chip = me_h // 2
    sibling = me_h + 1 - 2 * core

    def cpeer(r):
        return lax.rem(me_c + r, NC)

    def hpeer(r):
        return lax.rem(me_h + r, NH)

    def remote(src, dst, s, axis, to):
        pltpu.make_async_remote_copy(
            src_ref=src, dst_ref=dst, send_sem=send.at[s], recv_sem=recv.at[s],
            device_id={axis: to}, device_id_type=MESH,
        ).start()

    def local(src, dst, s):
        pltpu.make_async_copy(src, dst, recv.at[s]).start()

    def arrived(ref, s):
        pltpu.make_async_copy(ref, ref, recv.at[s]).wait()

    def left(ref, s):
        pltpu.make_async_copy(ref, ref, send.at[s]).wait()

    def block(k):
        return pl.ds(pl.multiple_of(k * TOK, TOK), TOK)

    def heads(k):
        return pl.ds(pl.multiple_of(k * GH, GH), GH)

    barrier = pltpu.get_barrier_semaphore()

    def greet_head(r, z):
        pl.semaphore_signal(barrier, inc=1, device_id={"head": hpeer(r)}, device_id_type=MESH)
        return z

    def greet_ctx(r, z):
        pl.semaphore_signal(barrier, inc=1, device_id={"ctx": cpeer(r)}, device_id_type=MESH)
        return z

    lax.fori_loop(1, NH, greet_head, 0)
    lax.fori_loop(1, NC, greet_ctx, 0)

    local(st, own.at[pl.ds(0, TOK), :], 24)
    local(ld, own.at[pl.ds(TOK, TOK), :], 24)
    rep_one = ones_where(iota((N, W), 0) == iota((N, W), 1) // HD)
    rep[0:N, :] = rep_one
    rep[N : 2 * N, :] = rep_one
    row, col = iota((Q, Q), 0), iota((Q, Q), 1)
    tri[...] = ones_where(row >= col)
    below = row >= col
    above = row <= col
    skip_hi = skip[...].astype(BF)
    skip_mid, skip_low = halves(skip[...] - skip_hi.astype(F32))
    skip_row = (
        dot(skip_hi, rep[0:GH, :]) + dot(skip_mid, rep[0:GH, :]) + dot(skip_low, rep[0:GH, :])
    )
    arrived(own, 24)
    pki[...] = jnp.transpose(own[...].astype(F32)).astype(BF)

    pl.semaphore_wait(barrier, NH + NC - 2)

    mine = block(me_h)

    def send_small(r, z):
        to = hpeer(r)
        remote(pki.at[heads(to), :], pkr.at[heads(me_h), :], 0, "head", to)
        return z

    lax.fori_loop(1, NH, send_small, 0)
    local(pki.at[heads(me_h), :], pkr.at[heads(me_h), :], 0)

    def send_maps(to):
        remote(bm, sm.at[0, mine, :], 1, "head", to)
        remote(cm, sm.at[1, mine, :], 1, "head", to)

    def send_maps_chip(r, z):
        send_maps(2 * lax.rem(chip + r, CHIPS) + core)
        return z

    lax.fori_loop(1, CHIPS, send_maps_chip, 0)
    send_maps(sibling)
    local(bm, sm.at[0, mine, :], 1)
    local(cm, sm.at[1, mine, :], 1)

    def send_wide(src, dst, s, h):
        def cols(k):
            return pl.ds(pl.multiple_of(k * W + h * HW, HW), HW)

        half = pl.ds(h * HW, HW)

        def one(r, z):
            to = hpeer(r)
            remote(src.at[:, cols(to)], dst.at[mine, half], s, "head", to)
            return z

        lax.fori_loop(1, NH, one, 0)
        local(src.at[:, cols(me_h)], dst.at[mine, half], s)

    send_wide(g, gb, 3, 0)
    send_wide(g, gb, 4, 1)
    send_wide(x, xb, 5, 0)
    send_wide(x, xb, 6, 1)

    arrived(pkr, 0)
    turned = jnp.transpose(pkr[...].astype(F32)).astype(BF)
    for k in range(NH):
        part = dot(turned, ones_where((row == k * GH + col) & (col < GH)))
        stc[k * TOK : (k + 1) * TOK, :] = part[0:TOK, :]
        cumc[k * TOK : (k + 1) * TOK, :] = part[TOK:, :]
    tots = []
    for c in range(CH):
        at = slice(c * Q, (c + 1) * Q)
        cum = dot(tri[...], cumc[at, :].astype(BF))
        cumc[at, :] = cum
        tots.append(cum[Q - 1 : Q, :])
    upto = [tots[0]]
    for c in range(1, CH):
        upto.append(upto[-1] + tots[c])
    beyond = [None] * CH
    beyond[CH - 1] = jnp.zeros_like(tots[0])
    for c in range(CH - 2, -1, -1):
        beyond[c] = beyond[c + 1] + tots[c + 1]
    for k in range(CH):
        prod[k : k + 1, 0:N] = tots[k]
        prod[CH + k : CH + k + 1, 0:N] = upto[k]
        prod[2 * CH + k : 2 * CH + k + 1, 0:N] = beyond[k]
        prod[3 * CH + k : 3 * CH + k + 1, 0:N] = jnp.zeros_like(tots[0])
    rows = jnp.exp(prod[:, 0:N])
    hi = rows.astype(BF)
    mid, low = halves(rows - hi.astype(F32))
    rowf[...] = dot(jnp.concatenate([hi, mid], axis=1), rep[...]) + dot(low, rep[0:N, :])
    for a in range(LG):
        for h in range(2):
            lanes = slice(h * HW + a * N, h * HW + (a + 1) * N)
            dec[a, h] = rowf[2 * CH - 1 : 2 * CH, lanes]

    def send_decay(r, z):
        k = cpeer(r)
        remote(dec.at[k // RG], decr.at[me_c], 7, "ctx", k)
        return z

    lax.fori_loop(1, NC, send_decay, 0)
    local(dec.at[me_c // RG], decr.at[me_c], 7)

    arrived(sm.at[:, pl.ds(0, 5 * TOK), :], 1)

    def pass_maps(r, z):
        at = block(2 * lax.rem(chip + r, CHIPS) + core)
        remote(sm.at[:, at, :], sm.at[:, at, :], 2, "head", sibling)
        return z

    lax.fori_loop(1, CHIPS, pass_maps, 0)

    def chunk(c):
        return pl.ds(pl.multiple_of(c * Q, Q), Q)

    def expand(a):
        return dot(jnp.concatenate(halves(a), axis=1), rep[...])

    for c in range(CH):
        at = slice(c * Q, (c + 1) * Q)
        cum = cumc[at, :]
        s = stc[at, :]
        f1[at, :] = expand(jnp.exp(cum))
        f2[at, :] = expand(s * jnp.exp(-cum))
        f1d[at, :] = expand(jnp.exp(cum + (upto[c] - tots[c])))
        f2d[at, :] = expand(s * jnp.exp(tots[c] - cum + beyond[c]))

    arrived(sm.at[:, pl.ds(0, 3 * TOK), :], 2)

    def transposed(a, out, c):
        t = jnp.transpose(a.astype(F32)).astype(BF)
        out[c, :, 0:Q] = t
        out[c, :, Q : 2 * Q] = t

    for c in range(CH):
        at = slice(c * Q, (c + 1) * Q)
        transposed(sm[0, at, :], bt2, c)
        transposed(sm[1, at, :], ct2, c)

    def stage(src, dst, h):
        for k in range(NC):
            a, b = k % RG * RB, h * HW + k // RG * N
            dst[h, k] = src[a : a + RB, b : b + N].astype(dst.dtype)

    def unstage(src, dst, h):
        for k in range(NC):
            a, b = k % RG * RB, h * HW + k // RG * N
            dst[a : a + RB, b : b + N] = src[h, k]

    def spread(src, dst, s, h):
        def one(r, z):
            k = cpeer(r)
            remote(src.at[h, k], dst.at[h, me_c], s + h, "ctx", k)
            return z

        lax.fori_loop(1, NC, one, 0)
        local(src.at[h, me_c], dst.at[h, me_c], s + h)

    def half_of(h):
        return slice(h * HW, (h + 1) * HW)

    def local_u(h):
        half = half_of(h)

        def step_u(c, z):
            at = chunk(c)
            b = sm[0, at, :]
            cb = jnp.where(above, dot(b, sm[1, at, :], NT), 0.0).astype(BF)
            v[at, half] = f2[at, half] * dot(jnp.concatenate([cb, b], axis=1), gx[c, :, half])
            return z

        lax.fori_loop(0, CH, step_u, 0)

    def owners_g(h):
        arrived(gr.at[h], 8 + h)

        def back_g(r, carry):
            i = NC - 1 - r
            gbs[h, i] = carry.astype(BF)
            gf32[h, i] = carry
            return carry * decr[i, h] + gr[h, i].astype(F32)

        lax.fori_loop(0, NC, back_g, jnp.zeros((RB, N), F32))
        spread(gbs, gbr, 10, h)

    def local_g(h):
        half = half_of(h)
        arrived(gb.at[:, pl.ds(h * HW, HW)], 3 + h)
        acc[:, half] = jnp.zeros((N, HW), F32)

        def step_g(r, z):
            c = CH - 1 - r
            at = chunk(c)
            ghi, glo = halves(gb[at, half].astype(F32) * f1[at, half])
            gx[c, 0:Q, half] = ghi
            end = acc[:, half]
            lg[c, :, half] = end
            end = end * rowf[pl.ds(c, 1), half]
            gx[c, Q : 2 * Q, half] = end.astype(BF)
            acc[:, half] = end + dot(ct2[c], jnp.concatenate([ghi, glo], axis=0))
            return z

        lax.fori_loop(0, CH, step_g, 0)
        stage(acc, gs, h)
        spread(gs, gr, 8, h)

    def local_x(h):
        half = half_of(h)
        arrived(xb.at[:, pl.ds(h * HW, HW)], 5 + h)
        acc[:, half] = jnp.zeros((N, HW), F32)

        def step_x(c, z):
            at = chunk(c)
            xhi, xlo = halves(xb[at, half].astype(F32) * f2[at, half])
            xs[c, 0:Q, half] = xhi
            start = acc[:, half]
            ls[c, :, half] = start
            xs[c, Q : 2 * Q, half] = start.astype(BF)
            more = dot(bt2[c], jnp.concatenate([xhi, xlo], axis=0))
            acc[:, half] = (start + more) * rowf[pl.ds(c, 1), half]
            return z

        lax.fori_loop(0, CH, step_x, 0)
        ls[CH, :, half] = acc[:, half]
        stage(acc, ss, h)
        spread(ss, sr, 12, h)

    def channels(h):
        half = half_of(h)
        arrived(gbr.at[h], 10 + h)
        unstage(gbr, gin, h)
        there = pl.ds(pl.multiple_of(me_h * W + h * HW, HW), HW)

        def make_dx(p):
            at = chunk(p)
            now = v[at, half] + f2d[at, half] * dot(sm[0, at, :], gin[:, half])
            v[at, half] = now
            dxb[at, half] = (now + skip_row[:, half] * gb[at, half].astype(F32)).astype(BF)

        def send_dx(to):
            remote(dxb.at[block(to), pl.ds(h * HW, HW)], ox.at[:, there], 18, "head", to)

        def step_dx(r, z):
            p = lax.rem(chip + r, CHIPS)
            make_dx(p)
            send_dx(2 * p)
            send_dx(2 * p + 1)
            return z

        lax.fori_loop(1, CHIPS, step_dx, 0)
        make_dx(chip)
        send_dx(sibling)
        local(dxb.at[mine, pl.ds(h * HW, HW)], ox.at[:, there], 18)

    def owners_s(h):
        arrived(sr.at[h], 12 + h)

        def back_s(i, carry):
            sbs[h, i] = carry.astype(BF)
            pairs[i, h] = jnp.sum(carry * gf32[h, i], axis=0, keepdims=True)
            return carry * decr[i, h] + sr[h, i].astype(F32)

        lax.fori_loop(0, NC, back_s, jnp.zeros((RB, N), F32))
        spread(sbs, sbr, 14, h)

    local_g(0)
    local_u(0)
    local_g(1)
    arrived(decr, 7)
    owners_g(0)
    local_u(1)
    owners_g(1)
    local_x(0)
    channels(0)
    local_x(1)
    channels(1)
    owners_s(0)
    owners_s(1)

    def send_pairs(r, z):
        k = cpeer(r)
        remote(pairs.at[k], pairr.at[me_c], 16, "ctx", k)
        return z

    lax.fori_loop(1, NC, send_pairs, 0)
    local(pairs.at[me_c], pairr.at[me_c], 16)

    def heads_sum(a, half=slice(0, W)):
        hi, lo = halves(a)
        return dot(hi, rep[0:N, half], NT) + dot(lo, rep[0:N, half], NT)

    def step_local(c, z):
        at = chunk(c)
        b, cc = sm[0, at, :], sm[1, at, :]
        gh, xh = gx[c, 0:Q, :], xs[c, 0:Q, :]
        xf, gf = xb[at, :].astype(F32), gb[at, :].astype(F32)
        cs[at, :] = heads_sum(xf * v[at, :])
        e = jnp.where(below, dot(gh, xh, NT), 0.0).astype(BF)
        et = jnp.where(above, dot(xh, gh, NT), 0.0).astype(BF)
        gk = (
            dot(et, cc)
            + dot(xh, gx[c, Q : 2 * Q, :], NT)
            + dot((xf * f2d[at, :]).astype(BF), gin[...], NT)
        )
        gq = dot(e, b) + dot(gh, xs[c, Q : 2 * Q, :], NT)
        for k in range(2):
            gbp[c, k] = gk[k * TOK : (k + 1) * TOK, :]
            gcp[c, k] = gq[k * TOK : (k + 1) * TOK, :]
        cb = jnp.where(below, dot(cc, b, NT), 0.0).astype(BF)
        y = f1[at, :] * dot(jnp.concatenate([cb, cc], axis=1), xs[c])
        rs[at, :] = heads_sum(gf * y)
        return z

    lax.fori_loop(0, CH, step_local, 0)
    remote(gbp.at[:, 1 - core], gbo, 19, "head", sibling)

    def use_s(h):
        half = half_of(h)
        arrived(sbr.at[h], 14 + h)
        unstage(sbr, sin, h)

        def step_s(c, z):
            at = chunk(c)
            gd = gb[at, half].astype(F32) * f1d[at, half]
            gq = dot(gd.astype(BF), sin[:, half], NT)
            for k in range(2):
                now = gcp[c, k] + gq[k * TOK : (k + 1) * TOK, :]
                if h == 0:
                    gcp[c, k] = now
                else:
                    gcb[c, k] = now.astype(BF)
            rs[at, :] = rs[at, :] + heads_sum(gd * dot(sm[1, at, :], sin[:, half]), half)
            return z

        lax.fori_loop(0, CH, step_s, 0)

    use_s(0)
    arrived(gbo, 19)
    gbh[...] = gbp[:, pl.ds(core, 1)].reshape(CHIPS, TOK, N) + gbo[...]

    def send_gb(r, z):
        p = lax.rem(chip + r, CHIPS)
        remote(gbh.at[p], gbrv.at[chip], 20, "head", 2 * p + core)
        return z

    lax.fori_loop(1, CHIPS, send_gb, 0)
    local(gbh.at[chip], gbrv.at[chip], 20)

    use_s(1)

    def send_gc(r, z):
        to = hpeer(r)
        remote(gcb.at[to // 2, lax.rem(to, 2)], gcrv.at[me_h], 21, "head", to)
        return z

    lax.fori_loop(1, NH, send_gc, 0)
    local(gcb.at[chip, core], gcrv.at[me_h], 21)

    arrived(pairr, 16)
    gi, si = gin[...].astype(F32), sin[...].astype(F32)
    exact = []
    for h in range(2):
        for a in range(LG):
            exact.append(jnp.sum(pairr[a * RG : (a + 1) * RG, h], axis=0))
    fix = rowf[2 * CH - 1 : 2 * CH, :] * (
        jnp.concatenate(exact, axis=1) - jnp.sum(gi * si, axis=0, keepdims=True)
    )
    prod[...] = jnp.zeros_like(prod)
    for c in range(CH):
        ge = lg[c] + rowf[2 * CH + c : 2 * CH + c + 1, :] * gi
        se = ls[c + 1] + rowf[CH + c : CH + c + 1, :] * si
        prod[c : c + 1, :] = jnp.sum(ge * se, axis=0, keepdims=True) + fix
    base = heads_sum(prod[...])
    lane = iota((Q, N), 1)
    upper = ones_where(above)
    packed = jnp.zeros((2 * TOK, N), F32)
    for c in range(CH):
        at = slice(c * Q, (c + 1) * Q)
        csum = cs[at, :]
        hi, lo = halves(rs[at, :] - csum)
        dq = base[c : c + 1, :] + dot(upper, hi) + dot(upper, lo)
        ds = jnp.where(lane < GH, csum / jnp.where(lane < GH, stc[at, :], 1.0), 0.0)
        for k in range(2):
            half = slice(k * TOK, (k + 1) * TOK)
            both = jnp.concatenate([ds[half, :], dq[half, :]], axis=0)
            turn = (2 * c + k) * GH
            packed = packed + (pltpu.roll(both, turn, 1) if turn else both)
    pko[...] = jnp.transpose(packed).astype(BF)

    def send_pk(r, z):
        to = hpeer(r)
        remote(pko.at[heads(to), :], pkv.at[heads(me_h), :], 23, "head", to)
        return z

    lax.fori_loop(1, NH, send_pk, 0)
    local(pko.at[heads(me_h), :], pkv.at[heads(me_h), :], 23)

    arrived(gbrv, 20)
    arrived(pkv, 23)
    arrived(gcrv, 21)
    arrived(ox, 18)

    left(pkr.at[pl.ds(0, N - GH), :], 0)
    left(sm.at[:, pl.ds(0, 4 * TOK), :], 1)
    left(sm.at[:, pl.ds(0, 3 * TOK), :], 2)
    for h in range(2):
        left(gb.at[pl.ds(0, LEN - TOK), pl.ds(0, HW)], 3 + h)
        left(xb.at[pl.ds(0, LEN - TOK), pl.ds(0, HW)], 5 + h)
        left(gs.at[h, pl.ds(0, NC - 1)], 8 + h)
        left(gbs.at[h, pl.ds(0, NC - 1)], 10 + h)
        left(ss.at[h, pl.ds(0, NC - 1)], 12 + h)
        left(sbs.at[h, pl.ds(0, NC - 1)], 14 + h)
    left(decr.at[pl.ds(0, NC - 1)], 7)
    left(pairr.at[pl.ds(0, NC - 1)], 16)
    left(dxb.at[pl.ds(0, LEN - TOK), :], 18)
    left(gbo, 19)
    left(gbh.at[pl.ds(0, CHIPS - 1)], 20)
    left(gcrv.at[pl.ds(0, NH - 1)], 21)
    left(pkv.at[pl.ds(0, N - GH), :], 23)


def finish(ox, pkv, gbrv, gcrv, odx, ods, odq, ogb, ogc, sem):
    move = pltpu.make_async_copy(ox, odx, sem)
    move.start()
    back = jnp.transpose(pkv[...].astype(F32)).astype(BF)
    ods[...] = back[0:TOK, :]
    odq[...] = back[TOK:, :]
    ogb[...] = jnp.sum(gbrv[...], axis=0)
    ogc[...] = jnp.sum(gcrv[...].astype(F32), axis=0)
    move.wait()


def body(inputs, grad_out, steps, log_decay, input_map, output_map, skip_gain):
    hbm = pl.BlockSpec(memory_space=pl.ANY)
    vmem = pl.BlockSpec(memory_space=pltpu.VMEM)

    def vm(shape, kind):
        return pltpu.VMEM(shape, kind)

    parts = pl.pallas_call(
        kernel,
        out_shape=(
            vm((TOK, NH * W), BF),
            vm((N, 2 * TOK), BF),
            vm((CHIPS, TOK, N), F32),
            vm((NH, TOK, N), BF),
        ),
        in_specs=[hbm] * 6 + [vmem],
        out_specs=(vmem,) * 4,
        scratch_shapes=[
            vm((LEN, W), BF),
            vm((LEN, W), BF),
            vm((2, LEN, N), BF),
            vm((2 * TOK, N), BF),
            vm((N, 2 * TOK), BF),
            vm((N, 2 * TOK), BF),
            vm((2 * N, W), BF),
            vm((LEN, W), F32),
            vm((LEN, W), F32),
            vm((LEN, W), F32),
            vm((LEN, W), F32),
            vm((4 * CH, W), F32),
            vm((Q, Q), BF),
            vm((LEN, N), F32),
            vm((LEN, N), F32),
            vm((CH, N, 2 * Q), BF),
            vm((CH, N, 2 * Q), BF),
            vm((CH, 2 * Q, W), BF),
            vm((CH, 2 * Q, W), BF),
            vm((CH, N, W), F32),
            vm((CH + 1, N, W), F32),
            vm((N, W), F32),
            vm((LEN, W), F32),
            vm((LEN, W), BF),
            vm((N, W), BF),
            vm((N, W), BF),
            vm((LG, 2, 1, N), F32),
            vm((NC, 2, 1, N), F32),
            vm((2, NC, RB, N), BF),
            vm((2, NC, RB, N), BF),
            vm((2, NC, RB, N), BF),
            vm((2, NC, RB, N), BF),
            vm((2, NC, RB, N), F32),
            vm((2, NC, RB, N), BF),
            vm((2, NC, RB, N), BF),
            vm((2, NC, RB, N), BF),
            vm((2, NC, RB, N), BF),
            vm((NC, 2, 1, N), F32),
            vm((NC, 2, 1, N), F32),
            vm((LEN, N), F32),
            vm((LEN, N), F32),
            vm((4 * CH, W), F32),
            vm((CHIPS, 2, TOK, N), F32),
            vm((CHIPS, 2, TOK, N), F32),
            vm((CHIPS, TOK, N), F32),
            vm((CHIPS, TOK, N), F32),
            vm((CHIPS, 2, TOK, N), BF),
            vm((N, 2 * TOK), BF),
            pltpu.SemaphoreType.DMA((24,)),
            pltpu.SemaphoreType.DMA((25,)),
        ],
        compiler_params=pltpu.CompilerParams(
            collective_id=0, has_side_effects=True, vmem_limit_bytes=56 * 1024 * 1024
        ),
        cost_estimate=pl.CostEstimate(
            flops=3 * 10**9, bytes_accessed=8 * 2**20, transcendentals=2**20
        ),
        name="block_backward",
    )(inputs, grad_out, steps, log_decay, input_map, output_map, skip_gain.reshape(1, GH))
    parts = [pltpu.with_memory_space_constraint(part, pltpu.VMEM) for part in parts]
    return pl.pallas_call(
        finish,
        out_shape=(
            jax.ShapeDtypeStruct((TOK, NH * W), BF),
            jax.ShapeDtypeStruct((TOK, N), BF),
            jax.ShapeDtypeStruct((TOK, N), BF),
            jax.ShapeDtypeStruct((TOK, N), F32),
            jax.ShapeDtypeStruct((TOK, N), F32),
        ),
        in_specs=[vmem] * 4,
        out_specs=(hbm, vmem, vmem, vmem, vmem),
        scratch_shapes=[pltpu.SemaphoreType.DMA],
        cost_estimate=pl.CostEstimate(flops=2**20, bytes_accessed=3 * 2**20, transcendentals=0),
        name="finish",
    )(*parts)


def solution(mesh):
    spread = P(("ctx", "head"), None)
    return jax.shard_map(
        body,
        mesh=mesh,
        in_specs=(spread,) * 6 + (P("head"),),
        out_specs=(spread,) * 5,
        check_vma=False,
    )
```

```python
import jax
import jax.numpy as jnp
from jax import lax
from jax.experimental import pallas as pl
from jax.experimental.pallas import tpu as pltpu
from jax.sharding import PartitionSpec as P

BF = jnp.bfloat16
F32 = jnp.float32
MESH = pl.DeviceIdType.MESH
NC = 32
NH = 8
TOK = 64
LEN = 512
Q = 128
CH = LEN // Q
W = 1024
HD = 64
N = 128
GH = 16
HW = W // 2
RB = 16
RG = N // RB
LG = HW // N
CHIPS = NH // 2
EARLY = 1

NN = ((1,), (0,))
NT = ((1,), (1,))


def dot(a, b, dims=NN):
    return lax.dot_general(a, b, (dims, ((), ())), preferred_element_type=F32)


def halves(a):
    hi = a.astype(BF)
    return hi, (a - hi.astype(F32)).astype(BF)


def iota(shape, axis):
    return lax.broadcasted_iota(jnp.int32, shape, axis)


def ones_where(cond):
    return jnp.where(cond, 1.0, 0.0).astype(BF)


def kernel(
    x, g, st, ld, bm, cm, skip, ox, pkv, gbrv, gcrv,
    gb, xb, sm, own, pki, pkr, rep, f1, f2, f1d, f2d, rowf, tri, stc, cumc, ct2, bt2, gx, xs,
    lg, ls, acc, v, dxb, gin, sin, dec, decr, gs, gr, gbs, gbr, gf32, ss, sr, sbs, sbr, pairs, pairr,
    cs, rs, prod, gbp, gcp, gbo, gbh, gcb, pko, send, recv,
):
    me_c = lax.axis_index("ctx")
    me_h = lax.axis_index("head")
    core = lax.rem(me_h, 2)
    chip = me_h // 2
    sibling = me_h + 1 - 2 * core

    def cpeer(r):
        return lax.rem(me_c + r, NC)

    def hpeer(r):
        return lax.rem(me_h + r, NH)

    def remote(src, dst, s, axis, to):
        pltpu.make_async_remote_copy(
            src_ref=src, dst_ref=dst, send_sem=send.at[s], recv_sem=recv.at[s],
            device_id={axis: to}, device_id_type=MESH,
        ).start()

    def local(src, dst, s):
        pltpu.make_async_copy(src, dst, recv.at[s]).start()

    def arrived(ref, s):
        pltpu.make_async_copy(ref, ref, recv.at[s]).wait()

    def left(ref, s):
        pltpu.make_async_copy(ref, ref, send.at[s]).wait()

    def block(k):
        return pl.ds(pl.multiple_of(k * TOK, TOK), TOK)

    def heads(k):
        return pl.ds(pl.multiple_of(k * GH, GH), GH)

    barrier = pltpu.get_barrier_semaphore()

    def greet_head(r, z):
        pl.semaphore_signal(barrier, inc=1, device_id={"head": hpeer(r)}, device_id_type=MESH)
        return z

    def greet_ctx(r, z):
        pl.semaphore_signal(barrier, inc=1, device_id={"ctx": cpeer(r)}, device_id_type=MESH)
        return z

    lax.fori_loop(1, NH, greet_head, 0)
    lax.fori_loop(1, NC, greet_ctx, 0)

    local(st, own.at[pl.ds(0, TOK), :], 24)
    local(ld, own.at[pl.ds(TOK, TOK), :], 24)
    rep_one = ones_where(iota((N, W), 0) == iota((N, W), 1) // HD)
    rep[0:N, :] = rep_one
    rep[N : 2 * N, :] = rep_one
    row, col = iota((Q, Q), 0), iota((Q, Q), 1)
    tri[...] = ones_where(row >= col)
    below = row >= col
    above = row <= col
    skip_hi = skip[...].astype(BF)
    skip_mid, skip_low = halves(skip[...] - skip_hi.astype(F32))
    skip_row = (
        dot(skip_hi, rep[0:GH, :]) + dot(skip_mid, rep[0:GH, :]) + dot(skip_low, rep[0:GH, :])
    )
    arrived(own, 24)
    pki[...] = jnp.transpose(own[...].astype(F32)).astype(BF)

    pl.semaphore_wait(barrier, NH + NC - 2)

    mine = block(me_h)

    def send_small(r, z):
        to = hpeer(r)
        remote(pki.at[heads(to), :], pkr.at[heads(me_h), :], 0, "head", to)
        return z

    lax.fori_loop(1, NH, send_small, 0)
    local(pki.at[heads(me_h), :], pkr.at[heads(me_h), :], 0)

    def send_maps(to):
        remote(bm, sm.at[0, mine, :], 1, "head", to)
        remote(cm, sm.at[1, mine, :], 1, "head", to)

    def send_maps_chip(r, z):
        send_maps(2 * lax.rem(chip + r, CHIPS) + core)
        return z

    lax.fori_loop(1, CHIPS, send_maps_chip, 0)
    send_maps(sibling)
    local(bm, sm.at[0, mine, :], 1)
    local(cm, sm.at[1, mine, :], 1)

    def send_wide(src, dst, s, h):
        def cols(k):
            return pl.ds(pl.multiple_of(k * W + h * HW, HW), HW)

        half = pl.ds(h * HW, HW)

        def one(r, z):
            to = hpeer(r)
            remote(src.at[:, cols(to)], dst.at[mine, half], s, "head", to)
            return z

        lax.fori_loop(1, NH, one, 0)
        local(src.at[:, cols(me_h)], dst.at[mine, half], s)

    send_wide(g, gb, 3, 0)
    send_wide(g, gb, 4, 1)
    send_wide(x, xb, 5, 0)
    send_wide(x, xb, 6, 1)

    arrived(pkr, 0)
    turned = jnp.transpose(pkr[...].astype(F32)).astype(BF)
    for k in range(NH):
        part = dot(turned, ones_where((row == k * GH + col) & (col < GH)))
        stc[k * TOK : (k + 1) * TOK, :] = part[0:TOK, :]
        cumc[k * TOK : (k + 1) * TOK, :] = part[TOK:, :]
    tots = []
    for c in range(CH):
        at = slice(c * Q, (c + 1) * Q)
        cum = dot(tri[...], cumc[at, :].astype(BF))
        cumc[at, :] = cum
        tots.append(cum[Q - 1 : Q, :])
    upto = [tots[0]]
    for c in range(1, CH):
        upto.append(upto[-1] + tots[c])
    beyond = [None] * CH
    beyond[CH - 1] = jnp.zeros_like(tots[0])
    for c in range(CH - 2, -1, -1):
        beyond[c] = beyond[c + 1] + tots[c + 1]
    for k in range(CH):
        prod[k : k + 1, 0:N] = tots[k]
        prod[CH + k : CH + k + 1, 0:N] = upto[k]
        prod[2 * CH + k : 2 * CH + k + 1, 0:N] = beyond[k]
        prod[3 * CH + k : 3 * CH + k + 1, 0:N] = jnp.zeros_like(tots[0])
    rows = jnp.exp(prod[:, 0:N])
    hi = rows.astype(BF)
    mid, low = halves(rows - hi.astype(F32))
    rowf[...] = dot(jnp.concatenate([hi, mid], axis=1), rep[...]) + dot(low, rep[0:N, :])
    for a in range(LG):
        for h in range(2):
            lanes = slice(h * HW + a * N, h * HW + (a + 1) * N)
            dec[a, h] = rowf[2 * CH - 1 : 2 * CH, lanes]

    def send_decay(r, z):
        k = cpeer(r)
        remote(dec.at[k // RG], decr.at[me_c], 7, "ctx", k)
        return z

    lax.fori_loop(1, NC, send_decay, 0)
    local(dec.at[me_c // RG], decr.at[me_c], 7)

    arrived(sm.at[:, pl.ds(0, 5 * TOK), :], 1)

    def pass_maps(r, z):
        at = block(2 * lax.rem(chip + r, CHIPS) + core)
        remote(sm.at[:, at, :], sm.at[:, at, :], 2, "head", sibling)
        return z

    lax.fori_loop(1, CHIPS, pass_maps, 0)

    def chunk(c):
        return pl.ds(pl.multiple_of(c * Q, Q), Q)

    def expand(a):
        return dot(jnp.concatenate(halves(a), axis=1), rep[...])

    for c in range(CH):
        at = slice(c * Q, (c + 1) * Q)
        cum = cumc[at, :]
        s = stc[at, :]
        f1[at, :] = expand(jnp.exp(cum))
        f2[at, :] = expand(s * jnp.exp(-cum))
        f1d[at, :] = expand(jnp.exp(cum + (upto[c] - tots[c])))
        f2d[at, :] = expand(s * jnp.exp(tots[c] - cum + beyond[c]))

    arrived(sm.at[:, pl.ds(0, 3 * TOK), :], 2)

    def transposed(a, out, c):
        t = jnp.transpose(a.astype(F32)).astype(BF)
        out[c, :, 0:Q] = t
        out[c, :, Q : 2 * Q] = t

    for c in range(CH):
        at = slice(c * Q, (c + 1) * Q)
        transposed(sm[0, at, :], bt2, c)
        transposed(sm[1, at, :], ct2, c)

    def stage(src, dst, h):
        for k in range(NC):
            a, b = k % RG * RB, h * HW + k // RG * N
            dst[h, k] = src[a : a + RB, b : b + N].astype(dst.dtype)

    def unstage(src, dst, h):
        for k in range(NC):
            a, b = k % RG * RB, h * HW + k // RG * N
            dst[a : a + RB, b : b + N] = src[h, k]

    def spread(src, dst, s, h):
        def one(r, z):
            k = cpeer(r)
            remote(src.at[h, k], dst.at[h, me_c], s + h, "ctx", k)
            return z

        lax.fori_loop(1, NC, one, 0)
        local(src.at[h, me_c], dst.at[h, me_c], s + h)

    def half_of(h):
        return slice(h * HW, (h + 1) * HW)

    def local_u(h):
        half = half_of(h)

        def step_u(c, z):
            at = chunk(c)
            b = sm[0, at, :]
            cb = jnp.where(above, dot(b, sm[1, at, :], NT), 0.0).astype(BF)
            v[at, half] = f2[at, half] * dot(jnp.concatenate([cb, b], axis=1), gx[c, :, half])
            return z

        lax.fori_loop(0, CH, step_u, 0)

    def owners_g(h):
        arrived(gr.at[h], 8 + h)

        def back_g(r, carry):
            i = NC - 1 - r
            gbs[h, i] = carry.astype(BF)
            gf32[h, i] = carry
            return carry * decr[i, h] + gr[h, i].astype(F32)

        lax.fori_loop(0, NC, back_g, jnp.zeros((RB, N), F32))
        spread(gbs, gbr, 10, h)

    def local_g(h):
        half = half_of(h)
        arrived(gb.at[:, pl.ds(h * HW, HW)], 3 + h)
        acc[:, half] = jnp.zeros((N, HW), F32)

        def step_g(r, z):
            c = CH - 1 - r
            at = chunk(c)
            ghi, glo = halves(gb[at, half].astype(F32) * f1[at, half])
            gx[c, 0:Q, half] = ghi
            end = acc[:, half]
            lg[c, :, half] = end
            end = end * rowf[pl.ds(c, 1), half]
            gx[c, Q : 2 * Q, half] = end.astype(BF)
            acc[:, half] = end + dot(ct2[c], jnp.concatenate([ghi, glo], axis=0))
            return z

        lax.fori_loop(0, CH, step_g, 0)
        stage(acc, gs, h)
        spread(gs, gr, 8, h)

    def local_x(h):
        half = half_of(h)
        arrived(xb.at[:, pl.ds(h * HW, HW)], 5 + h)
        acc[:, half] = jnp.zeros((N, HW), F32)

        def step_x(c, z):
            at = chunk(c)
            xhi, xlo = halves(xb[at, half].astype(F32) * f2[at, half])
            xs[c, 0:Q, half] = xhi
            start = acc[:, half]
            ls[c, :, half] = start
            xs[c, Q : 2 * Q, half] = start.astype(BF)
            more = dot(bt2[c], jnp.concatenate([xhi, xlo], axis=0))
            acc[:, half] = (start + more) * rowf[pl.ds(c, 1), half]
            return z

        lax.fori_loop(0, CH, step_x, 0)
        ls[CH, :, half] = acc[:, half]
        stage(acc, ss, h)
        spread(ss, sr, 12, h)

    def channels(h):
        half = half_of(h)
        arrived(gbr.at[h], 10 + h)
        unstage(gbr, gin, h)
        there = pl.ds(pl.multiple_of(me_h * W + h * HW, HW), HW)

        def make_dx(p):
            at = chunk(p)
            now = v[at, half] + f2d[at, half] * dot(sm[0, at, :], gin[:, half])
            v[at, half] = now
            dxb[at, half] = (now + skip_row[:, half] * gb[at, half].astype(F32)).astype(BF)

        def send_dx(to):
            remote(dxb.at[block(to), pl.ds(h * HW, HW)], ox.at[:, there], 18, "head", to)

        def step_dx(r, z):
            p = lax.rem(chip + r, CHIPS)
            make_dx(p)
            send_dx(2 * p)
            send_dx(2 * p + 1)
            return z

        lax.fori_loop(1, CHIPS, step_dx, 0)
        make_dx(chip)
        send_dx(sibling)
        local(dxb.at[mine, pl.ds(h * HW, HW)], ox.at[:, there], 18)

    def owners_s(h):
        arrived(sr.at[h], 12 + h)

        def back_s(i, carry):
            sbs[h, i] = carry.astype(BF)
            pairs[i, h] = jnp.sum(carry * gf32[h, i], axis=0, keepdims=True)
            return carry * decr[i, h] + sr[h, i].astype(F32)

        lax.fori_loop(0, NC, back_s, jnp.zeros((RB, N), F32))
        spread(sbs, sbr, 14, h)

    def heads_sum(a, half=slice(0, W)):
        hi, lo = halves(a)
        return dot(hi, rep[0:N, half], NT) + dot(lo, rep[0:N, half], NT)

    def step_local(c, z):
        at = chunk(c)
        b, cc = sm[0, at, :], sm[1, at, :]
        gh, xh = gx[c, 0:Q, :], xs[c, 0:Q, :]
        xf, gf = xb[at, :].astype(F32), gb[at, :].astype(F32)
        cs[at, :] = heads_sum(xf * v[at, :])
        e = jnp.where(below, dot(gh, xh, NT), 0.0).astype(BF)
        et = jnp.where(above, dot(xh, gh, NT), 0.0).astype(BF)
        gk = (
            dot(et, cc)
            + dot(xh, gx[c, Q : 2 * Q, :], NT)
            + dot((xf * f2d[at, :]).astype(BF), gin[...], NT)
        )
        gq = dot(e, b) + dot(gh, xs[c, Q : 2 * Q, :], NT)
        for k in range(2):
            gbp[c, k] = gk[k * TOK : (k + 1) * TOK, :]
            gcp[c, k] = gq[k * TOK : (k + 1) * TOK, :]
        cb = jnp.where(below, dot(cc, b, NT), 0.0).astype(BF)
        y = f1[at, :] * dot(jnp.concatenate([cb, cc], axis=1), xs[c])
        rs[at, :] = heads_sum(gf * y)
        return z

    local_g(0)
    local_u(0)
    local_g(1)
    arrived(decr, 7)
    owners_g(0)
    local_u(1)
    owners_g(1)
    local_x(0)
    channels(0)
    local_x(1)
    channels(1)
    lax.fori_loop(0, EARLY, step_local, 0)
    owners_s(0)
    owners_s(1)

    def send_pairs(r, z):
        k = cpeer(r)
        remote(pairs.at[k], pairr.at[me_c], 16, "ctx", k)
        return z

    lax.fori_loop(1, NC, send_pairs, 0)
    local(pairs.at[me_c], pairr.at[me_c], 16)

    lax.fori_loop(EARLY, CH, step_local, 0)
    remote(gbp.at[:, 1 - core], gbo, 19, "head", sibling)

    def use_s(h):
        half = half_of(h)
        arrived(sbr.at[h], 14 + h)
        unstage(sbr, sin, h)

        def use_chunk(c):
            at = chunk(c)
            gd = gb[at, half].astype(F32) * f1d[at, half]
            gq = dot(gd.astype(BF), sin[:, half], NT)
            for k in range(2):
                now = gcp[c, k] + gq[k * TOK : (k + 1) * TOK, :]
                if h == 0:
                    gcp[c, k] = now
                else:
                    gcb[c, k] = now.astype(BF)
            rs[at, :] = rs[at, :] + heads_sum(gd * dot(sm[1, at, :], sin[:, half]), half)

        def send_gc(c, k, to):
            remote(gcb.at[c, k], gcrv.at[me_h], 21, "head", to)

        def step_s(r, z):
            c = lax.rem(chip + r, CHIPS)
            use_chunk(c)
            if h == 1:
                send_gc(c, 0, 2 * c)
                send_gc(c, 1, 2 * c + 1)
            return z

        lax.fori_loop(1, CHIPS, step_s, 0)
        use_chunk(chip)
        if h == 1:
            send_gc(chip, 1 - core, sibling)
            local(gcb.at[chip, core], gcrv.at[me_h], 21)

    def pair_sums(h):
        half = half_of(h)
        gi, si = gin[:, half].astype(F32), sin[:, half].astype(F32)
        for c in range(CH):
            ge = lg[c, :, half] + rowf[2 * CH + c : 2 * CH + c + 1, half] * gi
            se = ls[c + 1, :, half] + rowf[CH + c : CH + c + 1, half] * si
            prod[c : c + 1, half] = jnp.sum(ge * se, axis=0, keepdims=True)
        prod[CH : CH + 1, half] = jnp.sum(gi * si, axis=0, keepdims=True)

    prod[...] = jnp.zeros_like(prod)
    use_s(0)
    pair_sums(0)
    arrived(gbo, 19)
    gbh[...] = gbp[:, pl.ds(core, 1)].reshape(CHIPS, TOK, N) + gbo[...]

    def send_gb(r, z):
        p = lax.rem(chip + r, CHIPS)
        remote(gbh.at[p], gbrv.at[chip], 20, "head", 2 * p + core)
        return z

    lax.fori_loop(1, CHIPS, send_gb, 0)
    local(gbh.at[chip], gbrv.at[chip], 20)

    use_s(1)

    pair_sums(1)
    arrived(pairr, 16)
    exact = []
    for h in range(2):
        for a in range(LG):
            exact.append(jnp.sum(pairr[a * RG : (a + 1) * RG, h], axis=0))
    fix = rowf[2 * CH - 1 : 2 * CH, :] * (
        jnp.concatenate(exact, axis=1) - prod[CH : CH + 1, :]
    )
    base = heads_sum(prod[...] + fix)
    lane = iota((Q, N), 1)
    upper = ones_where(above)
    packed = jnp.zeros((2 * TOK, N), F32)
    for c in range(CH):
        at = slice(c * Q, (c + 1) * Q)
        csum = cs[at, :]
        hi, lo = halves(rs[at, :] - csum)
        dq = base[c : c + 1, :] + dot(upper, hi) + dot(upper, lo)
        ds = jnp.where(lane < GH, csum / jnp.where(lane < GH, stc[at, :], 1.0), 0.0)
        for k in range(2):
            half = slice(k * TOK, (k + 1) * TOK)
            both = jnp.concatenate([ds[half, :], dq[half, :]], axis=0)
            turn = (2 * c + k) * GH
            packed = packed + (pltpu.roll(both, turn, 1) if turn else both)
    pko[...] = jnp.transpose(packed).astype(BF)

    def send_pk(r, z):
        to = hpeer(r)
        remote(pko.at[heads(to), :], pkv.at[heads(me_h), :], 23, "head", to)
        return z

    lax.fori_loop(1, NH, send_pk, 0)
    local(pko.at[heads(me_h), :], pkv.at[heads(me_h), :], 23)

    arrived(gbrv, 20)
    arrived(pkv, 23)
    arrived(gcrv, 21)
    arrived(ox, 18)

    left(pkr.at[pl.ds(0, N - GH), :], 0)
    left(sm.at[:, pl.ds(0, 4 * TOK), :], 1)
    left(sm.at[:, pl.ds(0, 3 * TOK), :], 2)
    for h in range(2):
        left(gb.at[pl.ds(0, LEN - TOK), pl.ds(0, HW)], 3 + h)
        left(xb.at[pl.ds(0, LEN - TOK), pl.ds(0, HW)], 5 + h)
        left(gs.at[h, pl.ds(0, NC - 1)], 8 + h)
        left(gbs.at[h, pl.ds(0, NC - 1)], 10 + h)
        left(ss.at[h, pl.ds(0, NC - 1)], 12 + h)
        left(sbs.at[h, pl.ds(0, NC - 1)], 14 + h)
    left(decr.at[pl.ds(0, NC - 1)], 7)
    left(pairr.at[pl.ds(0, NC - 1)], 16)
    left(dxb.at[pl.ds(0, LEN - TOK), :], 18)
    left(gbo, 19)
    left(gbh.at[pl.ds(0, CHIPS - 1)], 20)
    left(gcrv.at[pl.ds(0, NH - 1)], 21)
    left(pkv.at[pl.ds(0, N - GH), :], 23)


def finish(ox, pkv, gbrv, gcrv, odx, ods, odq, ogb, ogc, sem):
    move = pltpu.make_async_copy(ox, odx, sem)
    move.start()
    back = jnp.transpose(pkv[...].astype(F32)).astype(BF)
    ods[...] = back[0:TOK, :]
    odq[...] = back[TOK:, :]
    ogb[...] = jnp.sum(gbrv[...], axis=0)
    ogc[...] = jnp.sum(gcrv[...].astype(F32), axis=0)
    move.wait()


def body(inputs, grad_out, steps, log_decay, input_map, output_map, skip_gain):
    hbm = pl.BlockSpec(memory_space=pl.ANY)
    vmem = pl.BlockSpec(memory_space=pltpu.VMEM)

    def vm(shape, kind):
        return pltpu.VMEM(shape, kind)

    parts = pl.pallas_call(
        kernel,
        out_shape=(
            vm((TOK, NH * W), BF),
            vm((N, 2 * TOK), BF),
            vm((CHIPS, TOK, N), F32),
            vm((NH, TOK, N), BF),
        ),
        in_specs=[hbm] * 6 + [vmem],
        out_specs=(vmem,) * 4,
        scratch_shapes=[
            vm((LEN, W), BF),
            vm((LEN, W), BF),
            vm((2, LEN, N), BF),
            vm((2 * TOK, N), BF),
            vm((N, 2 * TOK), BF),
            vm((N, 2 * TOK), BF),
            vm((2 * N, W), BF),
            vm((LEN, W), F32),
            vm((LEN, W), F32),
            vm((LEN, W), F32),
            vm((LEN, W), F32),
            vm((4 * CH, W), F32),
            vm((Q, Q), BF),
            vm((LEN, N), F32),
            vm((LEN, N), F32),
            vm((CH, N, 2 * Q), BF),
            vm((CH, N, 2 * Q), BF),
            vm((CH, 2 * Q, W), BF),
            vm((CH, 2 * Q, W), BF),
            vm((CH, N, W), F32),
            vm((CH + 1, N, W), F32),
            vm((N, W), F32),
            vm((LEN, W), F32),
            vm((LEN, W), BF),
            vm((N, W), BF),
            vm((N, W), BF),
            vm((LG, 2, 1, N), F32),
            vm((NC, 2, 1, N), F32),
            vm((2, NC, RB, N), BF),
            vm((2, NC, RB, N), BF),
            vm((2, NC, RB, N), BF),
            vm((2, NC, RB, N), BF),
            vm((2, NC, RB, N), F32),
            vm((2, NC, RB, N), BF),
            vm((2, NC, RB, N), BF),
            vm((2, NC, RB, N), BF),
            vm((2, NC, RB, N), BF),
            vm((NC, 2, 1, N), F32),
            vm((NC, 2, 1, N), F32),
            vm((LEN, N), F32),
            vm((LEN, N), F32),
            vm((4 * CH, W), F32),
            vm((CHIPS, 2, TOK, N), F32),
            vm((CHIPS, 2, TOK, N), F32),
            vm((CHIPS, TOK, N), F32),
            vm((CHIPS, TOK, N), F32),
            vm((CHIPS, 2, TOK, N), BF),
            vm((N, 2 * TOK), BF),
            pltpu.SemaphoreType.DMA((24,)),
            pltpu.SemaphoreType.DMA((25,)),
        ],
        compiler_params=pltpu.CompilerParams(
            collective_id=0, has_side_effects=True, vmem_limit_bytes=56 * 1024 * 1024
        ),
        cost_estimate=pl.CostEstimate(
            flops=3 * 10**9, bytes_accessed=8 * 2**20, transcendentals=2**20
        ),
        name="block_backward",
    )(inputs, grad_out, steps, log_decay, input_map, output_map, skip_gain.reshape(1, GH))
    parts = [pltpu.with_memory_space_constraint(part, pltpu.VMEM) for part in parts]
    return pl.pallas_call(
        finish,
        out_shape=(
            jax.ShapeDtypeStruct((TOK, NH * W), BF),
            jax.ShapeDtypeStruct((TOK, N), BF),
            jax.ShapeDtypeStruct((TOK, N), BF),
            jax.ShapeDtypeStruct((TOK, N), F32),
            jax.ShapeDtypeStruct((TOK, N), F32),
        ),
        in_specs=[vmem] * 4,
        out_specs=(hbm, vmem, vmem, vmem, vmem),
        scratch_shapes=[pltpu.SemaphoreType.DMA],
        cost_estimate=pl.CostEstimate(flops=2**20, bytes_accessed=3 * 2**20, transcendentals=0),
        name="finish",
    )(*parts)


def solution(mesh):
    spread = P(("ctx", "head"), None)
    return jax.shard_map(
        body,
        mesh=mesh,
        in_specs=(spread,) * 6 + (P("head"),),
        out_specs=(spread,) * 5,
        check_vma=False,
    )
```

```python
import jax
import jax.numpy as jnp
from jax import lax
from jax.experimental import pallas as pl
from jax.experimental.pallas import tpu as pltpu
from jax.sharding import PartitionSpec as P

BF = jnp.bfloat16
F32 = jnp.float32
MESH = pl.DeviceIdType.MESH
NC = 32
NH = 8
TOK = 64
LEN = 512
Q = 128
CH = LEN // Q
W = 1024
HD = 64
N = 128
GH = 16
HW = W // 2
RB = 16
RG = N // RB
LG = HW // N
CHIPS = NH // 2
Z = 8
FAR_FIRST = sorted(range(1, NC), key=lambda r: (-min(r % Z, Z - r % Z), r))
EARLY = 1

NN = ((1,), (0,))
NT = ((1,), (1,))


def dot(a, b, dims=NN):
    return lax.dot_general(a, b, (dims, ((), ())), preferred_element_type=F32)


def halves(a):
    hi = a.astype(BF)
    return hi, (a - hi.astype(F32)).astype(BF)


def iota(shape, axis):
    return lax.broadcasted_iota(jnp.int32, shape, axis)


def ones_where(cond):
    return jnp.where(cond, 1.0, 0.0).astype(BF)


def kernel(
    x, g, st, ld, bm, cm, skip, ox, pkv, gbrv, gcrv,
    gb, xb, sm, own, pki, pkr, rep, f1, f2, f1d, f2d, rowf, tri, stc, cumc, ct2, bt2, gx, xs,
    lg, ls, acc, v, dxb, gin, sin, dec, decr, gs, gr, gbs, gbr, gf32, ss, sr, sbs, sbr, pairs, pairr,
    cs, rs, prod, gbp, gcp, gbo, gbh, gcb, pko, send, recv,
):
    me_c = lax.axis_index("ctx")
    me_h = lax.axis_index("head")
    core = lax.rem(me_h, 2)
    chip = me_h // 2
    sibling = me_h + 1 - 2 * core

    def cpeer(r):
        return lax.rem(me_c + r, NC)

    def hpeer(r):
        return lax.rem(me_h + r, NH)

    def remote(src, dst, s, axis, to):
        pltpu.make_async_remote_copy(
            src_ref=src, dst_ref=dst, send_sem=send.at[s], recv_sem=recv.at[s],
            device_id={axis: to}, device_id_type=MESH,
        ).start()

    def local(src, dst, s):
        pltpu.make_async_copy(src, dst, recv.at[s]).start()

    def arrived(ref, s):
        pltpu.make_async_copy(ref, ref, recv.at[s]).wait()

    def left(ref, s):
        pltpu.make_async_copy(ref, ref, send.at[s]).wait()

    def block(k):
        return pl.ds(pl.multiple_of(k * TOK, TOK), TOK)

    def heads(k):
        return pl.ds(pl.multiple_of(k * GH, GH), GH)

    barrier = pltpu.get_barrier_semaphore()

    def greet_head(r, z):
        pl.semaphore_signal(barrier, inc=1, device_id={"head": hpeer(r)}, device_id_type=MESH)
        return z

    def greet_ctx(r, z):
        pl.semaphore_signal(barrier, inc=1, device_id={"ctx": cpeer(r)}, device_id_type=MESH)
        return z

    lax.fori_loop(1, NH, greet_head, 0)
    lax.fori_loop(1, NC, greet_ctx, 0)

    local(st, own.at[pl.ds(0, TOK), :], 24)
    local(ld, own.at[pl.ds(TOK, TOK), :], 24)
    rep_one = ones_where(iota((N, W), 0) == iota((N, W), 1) // HD)
    rep[0:N, :] = rep_one
    rep[N : 2 * N, :] = rep_one
    row, col = iota((Q, Q), 0), iota((Q, Q), 1)
    tri[...] = ones_where(row >= col)
    below = row >= col
    above = row <= col
    skip_hi = skip[...].astype(BF)
    skip_mid, skip_low = halves(skip[...] - skip_hi.astype(F32))
    skip_row = (
        dot(skip_hi, rep[0:GH, :]) + dot(skip_mid, rep[0:GH, :]) + dot(skip_low, rep[0:GH, :])
    )
    arrived(own, 24)
    pki[...] = jnp.transpose(own[...].astype(F32)).astype(BF)

    pl.semaphore_wait(barrier, NH + NC - 2)

    mine = block(me_h)

    def send_small(r, z):
        to = hpeer(r)
        remote(pki.at[heads(to), :], pkr.at[heads(me_h), :], 0, "head", to)
        return z

    lax.fori_loop(1, NH, send_small, 0)
    local(pki.at[heads(me_h), :], pkr.at[heads(me_h), :], 0)

    def send_maps(to):
        remote(bm, sm.at[0, mine, :], 1, "head", to)
        remote(cm, sm.at[1, mine, :], 1, "head", to)

    def send_maps_chip(r, z):
        send_maps(2 * lax.rem(chip + r, CHIPS) + core)
        return z

    lax.fori_loop(1, CHIPS, send_maps_chip, 0)
    send_maps(sibling)
    local(bm, sm.at[0, mine, :], 1)
    local(cm, sm.at[1, mine, :], 1)

    def send_wide(src, dst, s, h):
        def cols(k):
            return pl.ds(pl.multiple_of(k * W + h * HW, HW), HW)

        half = pl.ds(h * HW, HW)

        def one(r, z):
            to = hpeer(r)
            remote(src.at[:, cols(to)], dst.at[mine, half], s, "head", to)
            return z

        lax.fori_loop(1, NH, one, 0)
        local(src.at[:, cols(me_h)], dst.at[mine, half], s)

    send_wide(g, gb, 3, 0)
    send_wide(g, gb, 4, 1)
    send_wide(x, xb, 5, 0)
    send_wide(x, xb, 6, 1)

    arrived(pkr, 0)
    turned = jnp.transpose(pkr[...].astype(F32)).astype(BF)
    for k in range(NH):
        part = dot(turned, ones_where((row == k * GH + col) & (col < GH)))
        stc[k * TOK : (k + 1) * TOK, :] = part[0:TOK, :]
        cumc[k * TOK : (k + 1) * TOK, :] = part[TOK:, :]
    tots = []
    for c in range(CH):
        at = slice(c * Q, (c + 1) * Q)
        cum = dot(tri[...], cumc[at, :].astype(BF))
        cumc[at, :] = cum
        tots.append(cum[Q - 1 : Q, :])
    upto = [tots[0]]
    for c in range(1, CH):
        upto.append(upto[-1] + tots[c])
    beyond = [None] * CH
    beyond[CH - 1] = jnp.zeros_like(tots[0])
    for c in range(CH - 2, -1, -1):
        beyond[c] = beyond[c + 1] + tots[c + 1]
    for k in range(CH):
        prod[k : k + 1, 0:N] = tots[k]
        prod[CH + k : CH + k + 1, 0:N] = upto[k]
        prod[2 * CH + k : 2 * CH + k + 1, 0:N] = beyond[k]
        prod[3 * CH + k : 3 * CH + k + 1, 0:N] = jnp.zeros_like(tots[0])
    rows = jnp.exp(prod[:, 0:N])
    hi = rows.astype(BF)
    mid, low = halves(rows - hi.astype(F32))
    rowf[...] = dot(jnp.concatenate([hi, mid], axis=1), rep[...]) + dot(low, rep[0:N, :])
    for a in range(LG):
        for h in range(2):
            lanes = slice(h * HW + a * N, h * HW + (a + 1) * N)
            dec[a, h] = rowf[2 * CH - 1 : 2 * CH, lanes]

    def send_decay(r, z):
        k = cpeer(r)
        remote(dec.at[k // RG], decr.at[me_c], 7, "ctx", k)
        return z

    lax.fori_loop(1, NC, send_decay, 0)
    local(dec.at[me_c // RG], decr.at[me_c], 7)

    arrived(sm.at[:, pl.ds(0, 5 * TOK), :], 1)

    def pass_maps(r, z):
        at = block(2 * lax.rem(chip + r, CHIPS) + core)
        remote(sm.at[:, at, :], sm.at[:, at, :], 2, "head", sibling)
        return z

    lax.fori_loop(1, CHIPS, pass_maps, 0)

    def chunk(c):
        return pl.ds(pl.multiple_of(c * Q, Q), Q)

    def expand(a):
        return dot(jnp.concatenate(halves(a), axis=1), rep[...])

    for c in range(CH):
        at = slice(c * Q, (c + 1) * Q)
        cum = cumc[at, :]
        s = stc[at, :]
        f1[at, :] = expand(jnp.exp(cum))
        f2[at, :] = expand(s * jnp.exp(-cum))
        f1d[at, :] = expand(jnp.exp(cum + (upto[c] - tots[c])))
        f2d[at, :] = expand(s * jnp.exp(tots[c] - cum + beyond[c]))

    arrived(sm.at[:, pl.ds(0, 3 * TOK), :], 2)

    def transposed(a, out, c):
        t = jnp.transpose(a.astype(F32)).astype(BF)
        out[c, :, 0:Q] = t
        out[c, :, Q : 2 * Q] = t

    for c in range(CH):
        at = slice(c * Q, (c + 1) * Q)
        transposed(sm[0, at, :], bt2, c)
        transposed(sm[1, at, :], ct2, c)

    def stage(src, dst, h):
        for k in range(NC):
            a, b = k % RG * RB, h * HW + k // RG * N
            dst[h, k] = src[a : a + RB, b : b + N].astype(dst.dtype)

    def unstage(src, dst, h):
        for k in range(NC):
            a, b = k % RG * RB, h * HW + k // RG * N
            dst[a : a + RB, b : b + N] = src[h, k]

    def spread(src, dst, s, h):
        for r in FAR_FIRST:
            k = cpeer(r)
            remote(src.at[h, k], dst.at[h, me_c], s + h, "ctx", k)
        local(src.at[h, me_c], dst.at[h, me_c], s + h)

    def half_of(h):
        return slice(h * HW, (h + 1) * HW)

    def local_u(h):
        half = half_of(h)

        def step_u(c, z):
            at = chunk(c)
            b = sm[0, at, :]
            cb = jnp.where(above, dot(b, sm[1, at, :], NT), 0.0).astype(BF)
            v[at, half] = f2[at, half] * dot(jnp.concatenate([cb, b], axis=1), gx[c, :, half])
            return z

        lax.fori_loop(0, CH, step_u, 0)

    def owners_g(h):
        arrived(gr.at[h], 8 + h)

        def back_g(r, carry):
            i = NC - 1 - r
            gbs[h, i] = carry.astype(BF)
            gf32[h, i] = carry
            return carry * decr[i, h] + gr[h, i].astype(F32)

        lax.fori_loop(0, NC, back_g, jnp.zeros((RB, N), F32))
        spread(gbs, gbr, 10, h)

    def local_g(h):
        half = half_of(h)
        arrived(gb.at[:, pl.ds(h * HW, HW)], 3 + h)
        acc[:, half] = jnp.zeros((N, HW), F32)

        def step_g(r, z):
            c = CH - 1 - r
            at = chunk(c)
            ghi, glo = halves(gb[at, half].astype(F32) * f1[at, half])
            gx[c, 0:Q, half] = ghi
            end = acc[:, half]
            lg[c, :, half] = end
            end = end * rowf[pl.ds(c, 1), half]
            gx[c, Q : 2 * Q, half] = end.astype(BF)
            acc[:, half] = end + dot(ct2[c], jnp.concatenate([ghi, glo], axis=0))
            return z

        lax.fori_loop(0, CH, step_g, 0)
        stage(acc, gs, h)
        spread(gs, gr, 8, h)

    def local_x(h):
        half = half_of(h)
        arrived(xb.at[:, pl.ds(h * HW, HW)], 5 + h)
        acc[:, half] = jnp.zeros((N, HW), F32)

        def step_x(c, z):
            at = chunk(c)
            xhi, xlo = halves(xb[at, half].astype(F32) * f2[at, half])
            xs[c, 0:Q, half] = xhi
            start = acc[:, half]
            ls[c, :, half] = start
            xs[c, Q : 2 * Q, half] = start.astype(BF)
            more = dot(bt2[c], jnp.concatenate([xhi, xlo], axis=0))
            acc[:, half] = (start + more) * rowf[pl.ds(c, 1), half]
            return z

        lax.fori_loop(0, CH, step_x, 0)
        ls[CH, :, half] = acc[:, half]
        stage(acc, ss, h)
        spread(ss, sr, 12, h)

    def channels(h):
        half = half_of(h)
        arrived(gbr.at[h], 10 + h)
        unstage(gbr, gin, h)
        there = pl.ds(pl.multiple_of(me_h * W + h * HW, HW), HW)

        def make_dx(p):
            at = chunk(p)
            now = v[at, half] + f2d[at, half] * dot(sm[0, at, :], gin[:, half])
            v[at, half] = now
            dxb[at, half] = (now + skip_row[:, half] * gb[at, half].astype(F32)).astype(BF)

        def send_dx(to):
            remote(dxb.at[block(to), pl.ds(h * HW, HW)], ox.at[:, there], 18, "head", to)

        def step_dx(r, z):
            p = lax.rem(chip + r, CHIPS)
            make_dx(p)
            send_dx(2 * p)
            send_dx(2 * p + 1)
            return z

        lax.fori_loop(1, CHIPS, step_dx, 0)
        make_dx(chip)
        send_dx(sibling)
        local(dxb.at[mine, pl.ds(h * HW, HW)], ox.at[:, there], 18)

    def owners_s(h):
        arrived(sr.at[h], 12 + h)

        def back_s(i, carry):
            sbs[h, i] = carry.astype(BF)
            pairs[i, h] = jnp.sum(carry * gf32[h, i], axis=0, keepdims=True)
            return carry * decr[i, h] + sr[h, i].astype(F32)

        lax.fori_loop(0, NC, back_s, jnp.zeros((RB, N), F32))
        spread(sbs, sbr, 14, h)

    def heads_sum(a, half=slice(0, W)):
        hi, lo = halves(a)
        return dot(hi, rep[0:N, half], NT) + dot(lo, rep[0:N, half], NT)

    def step_local(c, z):
        at = chunk(c)
        b, cc = sm[0, at, :], sm[1, at, :]
        gh, xh = gx[c, 0:Q, :], xs[c, 0:Q, :]
        xf, gf = xb[at, :].astype(F32), gb[at, :].astype(F32)
        cs[at, :] = heads_sum(xf * v[at, :])
        e = jnp.where(below, dot(gh, xh, NT), 0.0).astype(BF)
        et = jnp.where(above, dot(xh, gh, NT), 0.0).astype(BF)
        gk = (
            dot(et, cc)
            + dot(xh, gx[c, Q : 2 * Q, :], NT)
            + dot((xf * f2d[at, :]).astype(BF), gin[...], NT)
        )
        gq = dot(e, b) + dot(gh, xs[c, Q : 2 * Q, :], NT)
        for k in range(2):
            gbp[c, k] = gk[k * TOK : (k + 1) * TOK, :]
            gcp[c, k] = gq[k * TOK : (k + 1) * TOK, :]
        cb = jnp.where(below, dot(cc, b, NT), 0.0).astype(BF)
        y = f1[at, :] * dot(jnp.concatenate([cb, cc], axis=1), xs[c])
        rs[at, :] = heads_sum(gf * y)
        return z

    local_g(0)
    local_u(0)
    local_g(1)
    arrived(decr, 7)
    owners_g(0)
    local_u(1)
    owners_g(1)
    local_x(0)
    channels(0)
    local_x(1)
    channels(1)
    lax.fori_loop(0, EARLY, step_local, 0)
    owners_s(0)
    owners_s(1)

    def send_pairs(r, z):
        k = cpeer(r)
        remote(pairs.at[k], pairr.at[me_c], 16, "ctx", k)
        return z

    lax.fori_loop(1, NC, send_pairs, 0)
    local(pairs.at[me_c], pairr.at[me_c], 16)

    lax.fori_loop(EARLY, CH, step_local, 0)
    remote(gbp.at[:, 1 - core], gbo, 19, "head", sibling)

    def use_s(h):
        half = half_of(h)
        arrived(sbr.at[h], 14 + h)
        unstage(sbr, sin, h)

        def use_chunk(c):
            at = chunk(c)
            gd = gb[at, half].astype(F32) * f1d[at, half]
            gq = dot(gd.astype(BF), sin[:, half], NT)
            for k in range(2):
                now = gcp[c, k] + gq[k * TOK : (k + 1) * TOK, :]
                if h == 0:
                    gcp[c, k] = now
                else:
                    gcb[c, k] = now.astype(BF)
            rs[at, :] = rs[at, :] + heads_sum(gd * dot(sm[1, at, :], sin[:, half]), half)

        def send_gc(c, k, to):
            remote(gcb.at[c, k], gcrv.at[me_h], 21, "head", to)

        def step_s(r, z):
            c = lax.rem(chip + r, CHIPS)
            use_chunk(c)
            if h == 1:
                send_gc(c, 0, 2 * c)
                send_gc(c, 1, 2 * c + 1)
            return z

        lax.fori_loop(1, CHIPS, step_s, 0)
        use_chunk(chip)
        if h == 1:
            send_gc(chip, 1 - core, sibling)
            local(gcb.at[chip, core], gcrv.at[me_h], 21)

    def pair_sums(h):
        half = half_of(h)
        gi, si = gin[:, half].astype(F32), sin[:, half].astype(F32)
        for c in range(CH):
            ge = lg[c, :, half] + rowf[2 * CH + c : 2 * CH + c + 1, half] * gi
            se = ls[c + 1, :, half] + rowf[CH + c : CH + c + 1, half] * si
            prod[c : c + 1, half] = jnp.sum(ge * se, axis=0, keepdims=True)
        prod[CH : CH + 1, half] = jnp.sum(gi * si, axis=0, keepdims=True)

    prod[...] = jnp.zeros_like(prod)
    use_s(0)
    pair_sums(0)
    arrived(gbo, 19)
    gbh[...] = (gbp[:, pl.ds(core, 1)].reshape(CHIPS, TOK, N) + gbo[...]).astype(BF)

    def send_gb(r, z):
        p = lax.rem(chip + r, CHIPS)
        remote(gbh.at[p], gbrv.at[chip], 20, "head", 2 * p + core)
        return z

    lax.fori_loop(1, CHIPS, send_gb, 0)
    local(gbh.at[chip], gbrv.at[chip], 20)

    use_s(1)

    pair_sums(1)
    arrived(pairr, 16)
    exact = []
    for h in range(2):
        for a in range(LG):
            exact.append(jnp.sum(pairr[a * RG : (a + 1) * RG, h], axis=0))
    fix = rowf[2 * CH - 1 : 2 * CH, :] * (
        jnp.concatenate(exact, axis=1) - prod[CH : CH + 1, :]
    )
    base = heads_sum(prod[...] + fix)
    lane = iota((Q, N), 1)
    upper = ones_where(above)
    packed = jnp.zeros((2 * TOK, N), F32)
    for c in range(CH):
        at = slice(c * Q, (c + 1) * Q)
        csum = cs[at, :]
        hi, lo = halves(rs[at, :] - csum)
        dq = base[c : c + 1, :] + dot(upper, hi) + dot(upper, lo)
        ds = jnp.where(lane < GH, csum / jnp.where(lane < GH, stc[at, :], 1.0), 0.0)
        for k in range(2):
            half = slice(k * TOK, (k + 1) * TOK)
            both = jnp.concatenate([ds[half, :], dq[half, :]], axis=0)
            turn = (2 * c + k) * GH
            packed = packed + (pltpu.roll(both, turn, 1) if turn else both)
    pko[...] = jnp.transpose(packed).astype(BF)

    def send_pk(r, z):
        to = hpeer(r)
        remote(pko.at[heads(to), :], pkv.at[heads(me_h), :], 23, "head", to)
        return z

    lax.fori_loop(1, NH, send_pk, 0)
    local(pko.at[heads(me_h), :], pkv.at[heads(me_h), :], 23)

    arrived(gbrv, 20)
    arrived(pkv, 23)
    arrived(gcrv, 21)
    arrived(ox, 18)

    left(pkr.at[pl.ds(0, N - GH), :], 0)
    left(sm.at[:, pl.ds(0, 4 * TOK), :], 1)
    left(sm.at[:, pl.ds(0, 3 * TOK), :], 2)
    for h in range(2):
        left(gb.at[pl.ds(0, LEN - TOK), pl.ds(0, HW)], 3 + h)
        left(xb.at[pl.ds(0, LEN - TOK), pl.ds(0, HW)], 5 + h)
        left(gs.at[h, pl.ds(0, NC - 1)], 8 + h)
        left(gbs.at[h, pl.ds(0, NC - 1)], 10 + h)
        left(ss.at[h, pl.ds(0, NC - 1)], 12 + h)
        left(sbs.at[h, pl.ds(0, NC - 1)], 14 + h)
    left(decr.at[pl.ds(0, NC - 1)], 7)
    left(pairr.at[pl.ds(0, NC - 1)], 16)
    left(dxb.at[pl.ds(0, LEN - TOK), :], 18)
    left(gbo, 19)
    left(gbh.at[pl.ds(0, CHIPS - 1)], 20)
    left(gcrv.at[pl.ds(0, NH - 1)], 21)
    left(pkv.at[pl.ds(0, N - GH), :], 23)


def finish(ox, pkv, gbrv, gcrv, odx, ods, odq, ogb, ogc, sem):
    move = pltpu.make_async_copy(ox, odx, sem)
    move.start()
    back = jnp.transpose(pkv[...].astype(F32)).astype(BF)
    ods[...] = back[0:TOK, :]
    odq[...] = back[TOK:, :]
    ogb[...] = jnp.sum(gbrv[...].astype(F32), axis=0)
    ogc[...] = jnp.sum(gcrv[...].astype(F32), axis=0)
    move.wait()


def body(inputs, grad_out, steps, log_decay, input_map, output_map, skip_gain):
    hbm = pl.BlockSpec(memory_space=pl.ANY)
    vmem = pl.BlockSpec(memory_space=pltpu.VMEM)

    def vm(shape, kind):
        return pltpu.VMEM(shape, kind)

    parts = pl.pallas_call(
        kernel,
        out_shape=(
            vm((TOK, NH * W), BF),
            vm((N, 2 * TOK), BF),
            vm((CHIPS, TOK, N), BF),
            vm((NH, TOK, N), BF),
        ),
        in_specs=[hbm] * 6 + [vmem],
        out_specs=(vmem,) * 4,
        scratch_shapes=[
            vm((LEN, W), BF),
            vm((LEN, W), BF),
            vm((2, LEN, N), BF),
            vm((2 * TOK, N), BF),
            vm((N, 2 * TOK), BF),
            vm((N, 2 * TOK), BF),
            vm((2 * N, W), BF),
            vm((LEN, W), F32),
            vm((LEN, W), F32),
            vm((LEN, W), F32),
            vm((LEN, W), F32),
            vm((4 * CH, W), F32),
            vm((Q, Q), BF),
            vm((LEN, N), F32),
            vm((LEN, N), F32),
            vm((CH, N, 2 * Q), BF),
            vm((CH, N, 2 * Q), BF),
            vm((CH, 2 * Q, W), BF),
            vm((CH, 2 * Q, W), BF),
            vm((CH, N, W), F32),
            vm((CH + 1, N, W), F32),
            vm((N, W), F32),
            vm((LEN, W), F32),
            vm((LEN, W), BF),
            vm((N, W), BF),
            vm((N, W), BF),
            vm((LG, 2, 1, N), F32),
            vm((NC, 2, 1, N), F32),
            vm((2, NC, RB, N), BF),
            vm((2, NC, RB, N), BF),
            vm((2, NC, RB, N), BF),
            vm((2, NC, RB, N), BF),
            vm((2, NC, RB, N), F32),
            vm((2, NC, RB, N), BF),
            vm((2, NC, RB, N), BF),
            vm((2, NC, RB, N), BF),
            vm((2, NC, RB, N), BF),
            vm((NC, 2, 1, N), F32),
            vm((NC, 2, 1, N), F32),
            vm((LEN, N), F32),
            vm((LEN, N), F32),
            vm((4 * CH, W), F32),
            vm((CHIPS, 2, TOK, N), F32),
            vm((CHIPS, 2, TOK, N), F32),
            vm((CHIPS, TOK, N), F32),
            vm((CHIPS, TOK, N), BF),
            vm((CHIPS, 2, TOK, N), BF),
            vm((N, 2 * TOK), BF),
            pltpu.SemaphoreType.DMA((24,)),
            pltpu.SemaphoreType.DMA((25,)),
        ],
        compiler_params=pltpu.CompilerParams(
            collective_id=0, has_side_effects=True, vmem_limit_bytes=56 * 1024 * 1024
        ),
        cost_estimate=pl.CostEstimate(
            flops=3 * 10**9, bytes_accessed=8 * 2**20, transcendentals=2**20
        ),
        name="block_backward",
    )(inputs, grad_out, steps, log_decay, input_map, output_map, skip_gain.reshape(1, GH))
    parts = [pltpu.with_memory_space_constraint(part, pltpu.VMEM) for part in parts]
    return pl.pallas_call(
        finish,
        out_shape=(
            jax.ShapeDtypeStruct((TOK, NH * W), BF),
            jax.ShapeDtypeStruct((TOK, N), BF),
            jax.ShapeDtypeStruct((TOK, N), BF),
            jax.ShapeDtypeStruct((TOK, N), F32),
            jax.ShapeDtypeStruct((TOK, N), F32),
        ),
        in_specs=[vmem] * 4,
        out_specs=(hbm, vmem, vmem, vmem, vmem),
        scratch_shapes=[pltpu.SemaphoreType.DMA],
        cost_estimate=pl.CostEstimate(flops=2**20, bytes_accessed=3 * 2**20, transcendentals=0),
        name="finish",
    )(*parts)


def solution(mesh):
    spread = P(("ctx", "head"), None)
    return jax.shard_map(
        body,
        mesh=mesh,
        in_specs=(spread,) * 6 + (P("head"),),
        out_specs=(spread,) * 5,
        check_vma=False,
    )
```

```python
import jax
import jax.numpy as jnp
from jax import lax
from jax.experimental import pallas as pl
from jax.experimental.pallas import tpu as pltpu
from jax.sharding import PartitionSpec as P

BF = jnp.bfloat16
F32 = jnp.float32
MESH = pl.DeviceIdType.MESH
NC = 32
NH = 8
TOK = 64
LEN = 512
Q = 128
CH = LEN // Q
W = 1024
HD = 64
N = 128
GH = 16
HW = W // 2
RB = 16
RG = N // RB
LG = HW // N
CHIPS = NH // 2
Z = 8
FAR_FIRST = sorted(range(1, NC), key=lambda r: (-min(r % Z, Z - r % Z), r))
EARLY = 1

NN = ((1,), (0,))
NT = ((1,), (1,))


def dot(a, b, dims=NN):
    return lax.dot_general(a, b, (dims, ((), ())), preferred_element_type=F32)


def halves(a):
    hi = a.astype(BF)
    return hi, (a - hi.astype(F32)).astype(BF)


def iota(shape, axis):
    return lax.broadcasted_iota(jnp.int32, shape, axis)


def ones_where(cond):
    return jnp.where(cond, 1.0, 0.0).astype(BF)


def kernel(
    x, g, st, ld, bm, cm, skip, ox, pkv, gbrv, gcrv,
    gb, xb, sm, own, pki, pkr, rep, f1, f2, f1d, f2d, rowf, tri, stc, cumc, ct2, bt2, gx, xs,
    lg, ls, acc, v, dxb, gin, sin, dec, decr, gs, gr, gbs, gbr, gf32, ss, sr, sbs, sbr, pairs, pairr,
    cs, rs, prod, gbp, gcp, gbo, gbh, gcb, pko, send, recv,
):
    me_c = lax.axis_index("ctx")
    me_h = lax.axis_index("head")
    core = lax.rem(me_h, 2)
    chip = me_h // 2
    sibling = me_h + 1 - 2 * core

    def cpeer(r):
        return lax.rem(me_c + r, NC)

    def hpeer(r):
        return lax.rem(me_h + r, NH)

    def remote(src, dst, s, axis, to):
        pltpu.make_async_remote_copy(
            src_ref=src, dst_ref=dst, send_sem=send.at[s], recv_sem=recv.at[s],
            device_id={axis: to}, device_id_type=MESH,
        ).start()

    def local(src, dst, s):
        pltpu.make_async_copy(src, dst, recv.at[s]).start()

    def arrived(ref, s):
        pltpu.make_async_copy(ref, ref, recv.at[s]).wait()

    def left(ref, s):
        pltpu.make_async_copy(ref, ref, send.at[s]).wait()

    def block(k):
        return pl.ds(pl.multiple_of(k * TOK, TOK), TOK)

    def heads(k):
        return pl.ds(pl.multiple_of(k * GH, GH), GH)

    barrier = pltpu.get_barrier_semaphore()

    def greet_head(r, z):
        pl.semaphore_signal(barrier, inc=1, device_id={"head": hpeer(r)}, device_id_type=MESH)
        return z

    def greet_ctx(r, z):
        pl.semaphore_signal(barrier, inc=1, device_id={"ctx": cpeer(r)}, device_id_type=MESH)
        return z

    lax.fori_loop(1, NH, greet_head, 0)
    lax.fori_loop(1, NC, greet_ctx, 0)

    local(st, own.at[pl.ds(0, TOK), :], 24)
    local(ld, own.at[pl.ds(TOK, TOK), :], 24)
    rep_one = ones_where(iota((N, W), 0) == iota((N, W), 1) // HD)
    rep[0:N, :] = rep_one
    rep[N : 2 * N, :] = rep_one
    row, col = iota((Q, Q), 0), iota((Q, Q), 1)
    tri[...] = ones_where(row >= col)
    below = row >= col
    above = row <= col
    skip_hi = skip[...].astype(BF)
    skip_mid, skip_low = halves(skip[...] - skip_hi.astype(F32))
    skip_row = (
        dot(skip_hi, rep[0:GH, :]) + dot(skip_mid, rep[0:GH, :]) + dot(skip_low, rep[0:GH, :])
    )
    arrived(own, 24)
    pki[...] = jnp.transpose(own[...].astype(F32)).astype(BF)

    pl.semaphore_wait(barrier, NH + NC - 2)

    mine = block(me_h)

    def send_small(r, z):
        to = hpeer(r)
        remote(pki.at[heads(to), :], pkr.at[heads(me_h), :], 0, "head", to)
        return z

    lax.fori_loop(1, NH, send_small, 0)
    local(pki.at[heads(me_h), :], pkr.at[heads(me_h), :], 0)

    def send_maps(to):
        remote(bm, sm.at[0, mine, :], 1, "head", to)
        remote(cm, sm.at[1, mine, :], 1, "head", to)

    def send_maps_chip(r, z):
        send_maps(2 * lax.rem(chip + r, CHIPS) + core)
        return z

    lax.fori_loop(1, CHIPS, send_maps_chip, 0)
    send_maps(sibling)
    local(bm, sm.at[0, mine, :], 1)
    local(cm, sm.at[1, mine, :], 1)

    def send_wide(src, dst, s, h):
        def cols(k):
            return pl.ds(pl.multiple_of(k * W + h * HW, HW), HW)

        half = pl.ds(h * HW, HW)

        def one(r, z):
            to = hpeer(r)
            remote(src.at[:, cols(to)], dst.at[mine, half], s, "head", to)
            return z

        lax.fori_loop(1, NH, one, 0)
        local(src.at[:, cols(me_h)], dst.at[mine, half], s)

    send_wide(g, gb, 3, 0)
    send_wide(g, gb, 4, 1)
    send_wide(x, xb, 5, 0)
    send_wide(x, xb, 6, 1)

    arrived(pkr, 0)
    turned = jnp.transpose(pkr[...].astype(F32)).astype(BF)
    for k in range(NH):
        part = dot(turned, ones_where((row == k * GH + col) & (col < GH)))
        stc[k * TOK : (k + 1) * TOK, :] = part[0:TOK, :]
        cumc[k * TOK : (k + 1) * TOK, :] = part[TOK:, :]
    tots = []
    for c in range(CH):
        at = slice(c * Q, (c + 1) * Q)
        cum = dot(tri[...], cumc[at, :].astype(BF))
        cumc[at, :] = cum
        tots.append(cum[Q - 1 : Q, :])
    upto = [tots[0]]
    for c in range(1, CH):
        upto.append(upto[-1] + tots[c])
    beyond = [None] * CH
    beyond[CH - 1] = jnp.zeros_like(tots[0])
    for c in range(CH - 2, -1, -1):
        beyond[c] = beyond[c + 1] + tots[c + 1]
    for k in range(CH):
        prod[k : k + 1, 0:N] = tots[k]
        prod[CH + k : CH + k + 1, 0:N] = upto[k]
        prod[2 * CH + k : 2 * CH + k + 1, 0:N] = beyond[k]
        prod[3 * CH + k : 3 * CH + k + 1, 0:N] = jnp.zeros_like(tots[0])
    rows = jnp.exp(prod[:, 0:N])
    hi = rows.astype(BF)
    mid, low = halves(rows - hi.astype(F32))
    rowf[...] = dot(jnp.concatenate([hi, mid], axis=1), rep[...]) + dot(low, rep[0:N, :])
    for a in range(LG):
        for h in range(2):
            lanes = slice(h * HW + a * N, h * HW + (a + 1) * N)
            dec[a, h] = rowf[2 * CH - 1 : 2 * CH, lanes]

    def send_decay(r, z):
        k = cpeer(r)
        remote(dec.at[k // RG], decr.at[me_c], 7, "ctx", k)
        return z

    lax.fori_loop(1, NC, send_decay, 0)
    local(dec.at[me_c // RG], decr.at[me_c], 7)

    arrived(sm.at[:, pl.ds(0, 5 * TOK), :], 1)

    def pass_maps(r, z):
        at = block(2 * lax.rem(chip + r, CHIPS) + core)
        remote(sm.at[:, at, :], sm.at[:, at, :], 2, "head", sibling)
        return z

    lax.fori_loop(1, CHIPS, pass_maps, 0)

    def chunk(c):
        return pl.ds(pl.multiple_of(c * Q, Q), Q)

    def expand(a):
        return dot(jnp.concatenate(halves(a), axis=1), rep[...])

    for c in range(CH):
        at = slice(c * Q, (c + 1) * Q)
        cum = cumc[at, :]
        s = stc[at, :]
        f1[at, :] = expand(jnp.exp(cum))
        f2[at, :] = expand(s * jnp.exp(-cum))
        f1d[at, :] = expand(jnp.exp(cum + (upto[c] - tots[c])))
        f2d[at, :] = expand(s * jnp.exp(tots[c] - cum + beyond[c]))

    arrived(sm.at[:, pl.ds(0, 3 * TOK), :], 2)

    def transposed(a, out, c):
        t = jnp.transpose(a.astype(F32)).astype(BF)
        out[c, :, 0:Q] = t
        out[c, :, Q : 2 * Q] = t

    for c in range(CH):
        at = slice(c * Q, (c + 1) * Q)
        transposed(sm[0, at, :], bt2, c)
        transposed(sm[1, at, :], ct2, c)

    def stage(src, dst, h):
        for k in range(NC):
            a, b = k % RG * RB, h * HW + k // RG * N
            dst[h, k] = src[a : a + RB, b : b + N].astype(dst.dtype)

    def unstage(src, dst, h):
        for k in range(NC):
            a, b = k % RG * RB, h * HW + k // RG * N
            dst[a : a + RB, b : b + N] = src[h, k]

    def spread(src, dst, s, h):
        for r in FAR_FIRST:
            k = cpeer(r)
            remote(src.at[h, k], dst.at[h, me_c], s + h, "ctx", k)
        local(src.at[h, me_c], dst.at[h, me_c], s + h)

    def half_of(h):
        return slice(h * HW, (h + 1) * HW)

    def local_u(h):
        half = half_of(h)

        def step_u(c, z):
            at = chunk(c)
            b = sm[0, at, :]
            cb = jnp.where(above, dot(b, sm[1, at, :], NT), 0.0).astype(BF)
            v[at, half] = f2[at, half] * dot(jnp.concatenate([cb, b], axis=1), gx[c, :, half])
            return z

        lax.fori_loop(0, CH, step_u, 0)

    def owners_g(h):
        arrived(gr.at[h], 8 + h)

        def back_g(r, carry):
            i = NC - 1 - r
            gbs[h, i] = carry.astype(BF)
            gf32[h, i] = carry
            return carry * decr[i, h] + gr[h, i].astype(F32)

        lax.fori_loop(0, NC, back_g, jnp.zeros((RB, N), F32))
        spread(gbs, gbr, 10, h)

    def local_g(h):
        half = half_of(h)
        arrived(gb.at[:, pl.ds(h * HW, HW)], 3 + h)
        acc[:, half] = jnp.zeros((N, HW), F32)

        def step_g(r, z):
            c = CH - 1 - r
            at = chunk(c)
            ghi, glo = halves(gb[at, half].astype(F32) * f1[at, half])
            gx[c, 0:Q, half] = ghi
            end = acc[:, half]
            lg[c, :, half] = end
            end = end * rowf[pl.ds(c, 1), half]
            gx[c, Q : 2 * Q, half] = end.astype(BF)
            acc[:, half] = end + dot(ct2[c], jnp.concatenate([ghi, glo], axis=0))
            return z

        lax.fori_loop(0, CH, step_g, 0)
        stage(acc, gs, h)
        spread(gs, gr, 8, h)

    def local_x(h):
        half = half_of(h)
        arrived(xb.at[:, pl.ds(h * HW, HW)], 5 + h)
        acc[:, half] = jnp.zeros((N, HW), F32)

        def step_x(c, z):
            at = chunk(c)
            xhi, xlo = halves(xb[at, half].astype(F32) * f2[at, half])
            xs[c, 0:Q, half] = xhi
            start = acc[:, half]
            ls[c, :, half] = start
            xs[c, Q : 2 * Q, half] = start.astype(BF)
            more = dot(bt2[c], jnp.concatenate([xhi, xlo], axis=0))
            acc[:, half] = (start + more) * rowf[pl.ds(c, 1), half]
            return z

        lax.fori_loop(0, CH, step_x, 0)
        ls[CH, :, half] = acc[:, half]
        stage(acc, ss, h)
        spread(ss, sr, 12, h)

    def channels(h):
        half = half_of(h)
        arrived(gbr.at[h], 10 + h)
        unstage(gbr, gin, h)
        there = pl.ds(pl.multiple_of(me_h * W + h * HW, HW), HW)

        def make_dx(p):
            at = chunk(p)
            now = v[at, half] + f2d[at, half] * dot(sm[0, at, :], gin[:, half])
            v[at, half] = now
            dxb[at, half] = (now + skip_row[:, half] * gb[at, half].astype(F32)).astype(BF)

        def send_dx(to):
            remote(dxb.at[block(to), pl.ds(h * HW, HW)], ox.at[:, there], 18, "head", to)

        def step_dx(r, z):
            p = lax.rem(chip + r, CHIPS)
            make_dx(p)
            send_dx(2 * p)
            send_dx(2 * p + 1)
            return z

        lax.fori_loop(1, CHIPS, step_dx, 0)
        make_dx(chip)
        send_dx(sibling)
        local(dxb.at[mine, pl.ds(h * HW, HW)], ox.at[:, there], 18)

    def owners_s(h):
        arrived(sr.at[h], 12 + h)

        def back_s(i, carry):
            sbs[h, i] = carry.astype(BF)
            pairs[i, h] = jnp.sum(carry * gf32[h, i], axis=0, keepdims=True)
            return carry * decr[i, h] + sr[h, i].astype(F32)

        lax.fori_loop(0, NC, back_s, jnp.zeros((RB, N), F32))
        spread(sbs, sbr, 14, h)

    def heads_sum(a, half=slice(0, W)):
        hi, lo = halves(a)
        return dot(hi, rep[0:N, half], NT) + dot(lo, rep[0:N, half], NT)

    def step_local(c, z):
        at = chunk(c)
        b, cc = sm[0, at, :], sm[1, at, :]
        gh, xh = gx[c, 0:Q, :], xs[c, 0:Q, :]
        xf, gf = xb[at, :].astype(F32), gb[at, :].astype(F32)
        cs[at, :] = heads_sum(xf * v[at, :])
        e = jnp.where(below, dot(gh, xh, NT), 0.0).astype(BF)
        et = jnp.where(above, dot(xh, gh, NT), 0.0).astype(BF)
        gk = (
            dot(et, cc)
            + dot(xh, gx[c, Q : 2 * Q, :], NT)
            + dot((xf * f2d[at, :]).astype(BF), gin[...], NT)
        )
        gq = dot(e, b) + dot(gh, xs[c, Q : 2 * Q, :], NT)
        for k in range(2):
            gbp[c, k] = gk[k * TOK : (k + 1) * TOK, :]
            gcp[c, k] = gq[k * TOK : (k + 1) * TOK, :]
        cb = jnp.where(below, dot(cc, b, NT), 0.0).astype(BF)
        y = f1[at, :] * dot(jnp.concatenate([cb, cc], axis=1), xs[c])
        rs[at, :] = heads_sum(gf * y)
        return z

    local_g(0)
    local_u(0)
    local_g(1)
    arrived(decr, 7)
    owners_g(0)
    local_u(1)
    owners_g(1)
    local_x(0)
    local_x(1)
    channels(0)
    channels(1)
    lax.fori_loop(0, EARLY, step_local, 0)
    owners_s(0)
    owners_s(1)

    def send_pairs(r, z):
        k = cpeer(r)
        remote(pairs.at[k], pairr.at[me_c], 16, "ctx", k)
        return z

    lax.fori_loop(1, NC, send_pairs, 0)
    local(pairs.at[me_c], pairr.at[me_c], 16)

    lax.fori_loop(EARLY, CH, step_local, 0)
    remote(gbp.at[:, 1 - core], gbo, 19, "head", sibling)

    def use_s(h):
        half = half_of(h)
        arrived(sbr.at[h], 14 + h)
        unstage(sbr, sin, h)

        def use_chunk(c, leave):
            at = chunk(c)
            gd = gb[at, half].astype(F32) * f1d[at, half]
            gq = dot(gd.astype(BF), sin[:, half], NT)
            for k in range(2):
                now = gcp[c, k] + gq[k * TOK : (k + 1) * TOK, :]
                if h == 0:
                    gcp[c, k] = now
                else:
                    gcb[c, k] = now.astype(BF)
            if h == 1:
                leave(c)
            rs[at, :] = rs[at, :] + heads_sum(gd * dot(sm[1, at, :], sin[:, half]), half)

        def send_gc(c, k, to):
            remote(gcb.at[c, k], gcrv.at[me_h], 21, "head", to)

        def leave_far(c):
            send_gc(c, 0, 2 * c)
            send_gc(c, 1, 2 * c + 1)

        def leave_near(c):
            send_gc(c, 1 - core, sibling)
            local(gcb.at[c, core], gcrv.at[me_h], 21)

        def step_s(r, z):
            use_chunk(lax.rem(chip + r, CHIPS), leave_far)
            return z

        lax.fori_loop(1, CHIPS, step_s, 0)
        use_chunk(chip, leave_near)

    def pair_sums(h):
        half = half_of(h)
        gi, si = gin[:, half].astype(F32), sin[:, half].astype(F32)
        for c in range(CH):
            ge = lg[c, :, half] + rowf[2 * CH + c : 2 * CH + c + 1, half] * gi
            se = ls[c + 1, :, half] + rowf[CH + c : CH + c + 1, half] * si
            prod[c : c + 1, half] = jnp.sum(ge * se, axis=0, keepdims=True)
        prod[CH : CH + 1, half] = jnp.sum(gi * si, axis=0, keepdims=True)

    prod[...] = jnp.zeros_like(prod)
    use_s(0)
    pair_sums(0)
    arrived(gbo, 19)
    gbh[...] = (gbp[:, pl.ds(core, 1)].reshape(CHIPS, TOK, N) + gbo[...]).astype(BF)

    def send_gb(r, z):
        p = lax.rem(chip + r, CHIPS)
        remote(gbh.at[p], gbrv.at[chip], 20, "head", 2 * p + core)
        return z

    lax.fori_loop(1, CHIPS, send_gb, 0)
    local(gbh.at[chip], gbrv.at[chip], 20)

    use_s(1)

    pair_sums(1)
    arrived(pairr, 16)
    exact = []
    for h in range(2):
        for a in range(LG):
            exact.append(jnp.sum(pairr[a * RG : (a + 1) * RG, h], axis=0))
    fix = rowf[2 * CH - 1 : 2 * CH, :] * (
        jnp.concatenate(exact, axis=1) - prod[CH : CH + 1, :]
    )
    base = heads_sum(prod[...] + fix)
    lane = iota((Q, N), 1)
    upper = ones_where(above)
    packed = jnp.zeros((2 * TOK, N), F32)
    for c in range(CH):
        at = slice(c * Q, (c + 1) * Q)
        csum = cs[at, :]
        hi, lo = halves(rs[at, :] - csum)
        dq = base[c : c + 1, :] + dot(upper, hi) + dot(upper, lo)
        ds = jnp.where(lane < GH, csum / jnp.where(lane < GH, stc[at, :], 1.0), 0.0)
        for k in range(2):
            half = slice(k * TOK, (k + 1) * TOK)
            both = jnp.concatenate([ds[half, :], dq[half, :]], axis=0)
            turn = (2 * c + k) * GH
            packed = packed + (pltpu.roll(both, turn, 1) if turn else both)
    pko[...] = jnp.transpose(packed).astype(BF)

    def send_pk(r, z):
        to = hpeer(r)
        remote(pko.at[heads(to), :], pkv.at[heads(me_h), :], 23, "head", to)
        return z

    lax.fori_loop(1, NH, send_pk, 0)
    local(pko.at[heads(me_h), :], pkv.at[heads(me_h), :], 23)

    arrived(gbrv, 20)
    arrived(pkv, 23)
    arrived(gcrv, 21)
    arrived(ox, 18)

    left(pkr.at[pl.ds(0, N - GH), :], 0)
    left(sm.at[:, pl.ds(0, 4 * TOK), :], 1)
    left(sm.at[:, pl.ds(0, 3 * TOK), :], 2)
    for h in range(2):
        left(gb.at[pl.ds(0, LEN - TOK), pl.ds(0, HW)], 3 + h)
        left(xb.at[pl.ds(0, LEN - TOK), pl.ds(0, HW)], 5 + h)
        left(gs.at[h, pl.ds(0, NC - 1)], 8 + h)
        left(gbs.at[h, pl.ds(0, NC - 1)], 10 + h)
        left(ss.at[h, pl.ds(0, NC - 1)], 12 + h)
        left(sbs.at[h, pl.ds(0, NC - 1)], 14 + h)
    left(decr.at[pl.ds(0, NC - 1)], 7)
    left(pairr.at[pl.ds(0, NC - 1)], 16)
    left(dxb.at[pl.ds(0, LEN - TOK), :], 18)
    left(gbo, 19)
    left(gbh.at[pl.ds(0, CHIPS - 1)], 20)
    left(gcrv.at[pl.ds(0, NH - 1)], 21)
    left(pkv.at[pl.ds(0, N - GH), :], 23)


def finish(ox, pkv, gbrv, gcrv, odx, ods, odq, ogb, ogc, sem):
    move = pltpu.make_async_copy(ox, odx, sem)
    move.start()
    back = jnp.transpose(pkv[...].astype(F32)).astype(BF)
    ods[...] = back[0:TOK, :]
    odq[...] = back[TOK:, :]
    ogb[...] = jnp.sum(gbrv[...].astype(F32), axis=0)
    ogc[...] = jnp.sum(gcrv[...].astype(F32), axis=0)
    move.wait()


def body(inputs, grad_out, steps, log_decay, input_map, output_map, skip_gain):
    hbm = pl.BlockSpec(memory_space=pl.ANY)
    vmem = pl.BlockSpec(memory_space=pltpu.VMEM)

    def vm(shape, kind):
        return pltpu.VMEM(shape, kind)

    parts = pl.pallas_call(
        kernel,
        out_shape=(
            vm((TOK, NH * W), BF),
            vm((N, 2 * TOK), BF),
            vm((CHIPS, TOK, N), BF),
            vm((NH, TOK, N), BF),
        ),
        in_specs=[hbm] * 6 + [vmem],
        out_specs=(vmem,) * 4,
        scratch_shapes=[
            vm((LEN, W), BF),
            vm((LEN, W), BF),
            vm((2, LEN, N), BF),
            vm((2 * TOK, N), BF),
            vm((N, 2 * TOK), BF),
            vm((N, 2 * TOK), BF),
            vm((2 * N, W), BF),
            vm((LEN, W), F32),
            vm((LEN, W), F32),
            vm((LEN, W), F32),
            vm((LEN, W), F32),
            vm((4 * CH, W), F32),
            vm((Q, Q), BF),
            vm((LEN, N), F32),
            vm((LEN, N), F32),
            vm((CH, N, 2 * Q), BF),
            vm((CH, N, 2 * Q), BF),
            vm((CH, 2 * Q, W), BF),
            vm((CH, 2 * Q, W), BF),
            vm((CH, N, W), F32),
            vm((CH + 1, N, W), F32),
            vm((N, W), F32),
            vm((LEN, W), F32),
            vm((LEN, W), BF),
            vm((N, W), BF),
            vm((N, W), BF),
            vm((LG, 2, 1, N), F32),
            vm((NC, 2, 1, N), F32),
            vm((2, NC, RB, N), BF),
            vm((2, NC, RB, N), BF),
            vm((2, NC, RB, N), BF),
            vm((2, NC, RB, N), BF),
            vm((2, NC, RB, N), F32),
            vm((2, NC, RB, N), BF),
            vm((2, NC, RB, N), BF),
            vm((2, NC, RB, N), BF),
            vm((2, NC, RB, N), BF),
            vm((NC, 2, 1, N), F32),
            vm((NC, 2, 1, N), F32),
            vm((LEN, N), F32),
            vm((LEN, N), F32),
            vm((4 * CH, W), F32),
            vm((CHIPS, 2, TOK, N), F32),
            vm((CHIPS, 2, TOK, N), F32),
            vm((CHIPS, TOK, N), F32),
            vm((CHIPS, TOK, N), BF),
            vm((CHIPS, 2, TOK, N), BF),
            vm((N, 2 * TOK), BF),
            pltpu.SemaphoreType.DMA((24,)),
            pltpu.SemaphoreType.DMA((25,)),
        ],
        compiler_params=pltpu.CompilerParams(
            collective_id=0, has_side_effects=True, vmem_limit_bytes=56 * 1024 * 1024
        ),
        cost_estimate=pl.CostEstimate(
            flops=3 * 10**9, bytes_accessed=8 * 2**20, transcendentals=2**20
        ),
        name="block_backward",
    )(inputs, grad_out, steps, log_decay, input_map, output_map, skip_gain.reshape(1, GH))
    parts = [pltpu.with_memory_space_constraint(part, pltpu.VMEM) for part in parts]
    return pl.pallas_call(
        finish,
        out_shape=(
            jax.ShapeDtypeStruct((TOK, NH * W), BF),
            jax.ShapeDtypeStruct((TOK, N), BF),
            jax.ShapeDtypeStruct((TOK, N), BF),
            jax.ShapeDtypeStruct((TOK, N), F32),
            jax.ShapeDtypeStruct((TOK, N), F32),
        ),
        in_specs=[vmem] * 4,
        out_specs=(hbm, vmem, vmem, vmem, vmem),
        scratch_shapes=[pltpu.SemaphoreType.DMA],
        cost_estimate=pl.CostEstimate(flops=2**20, bytes_accessed=3 * 2**20, transcendentals=0),
        name="finish",
    )(*parts)


def solution(mesh):
    spread = P(("ctx", "head"), None)
    return jax.shard_map(
        body,
        mesh=mesh,
        in_specs=(spread,) * 6 + (P("head"),),
        out_specs=(spread,) * 5,
        check_vma=False,
    )
```
